128 devices in a mesh: row: 8 (over y_hi, z), col: 16 (over y_lo, x, core).
Axes of the slice: x: 4, y: 4 (y_hi: 2, y_lo: 2; y = y_hi * 2 + y_lo), z: 4, core: 2. Of those that a mesh axis runs over, the one named last changes fastest.
Arguments:
- left_tiles: bfloat16 [32, 4096, 256], P('row', 'col'), may hold values from 0.00049972534 to 0.049804688
- left_slots: int32 [32, 16], P('row', 'col'), may hold values from -1 to 7, as said below
- right_tiles: bfloat16 [32, 4096, 256], P('row', 'col'), may hold values from 0.00049972534 to 0.049804688
- right_slots: int32 [32, 16], P('row', 'col'), may hold values from -1 to 7, as said below
Outputs:
- inflated: float32 [16384, 16384], P('row', 'col')
The draws below stay inside these ranges and needn't reach their ends.
Inputs may be any that keep to these rules, and one draw needn't show every extreme that they name: `left_slots`: in each device's 4 slots the entries that are not -1 are distinct; half of the slots or more hold a tile, and some device holds a tile in every slot. `right_slots`: in each device's 4 slots the entries that are not -1 are distinct; half of the slots or more hold a tile, and some device holds a tile in every slot.
All inputs are finite; a program needn't handle non-finite values.
Results may differ from the reference program's by a relative error of at most 0.0003.
Values may be sent and summed in bfloat16 or wider, within the bound.
A program may use at most 192 MiB of HBM per device.

```python
import math
import jax
import jax.numpy as jnp

TILE = 256
RB_DEV = 8
CB_DEV = 4
KB_DEV = 1
KB_ALL = 16
KB_ROW = 2
CAP_A = 4
CAP_B = 4
ROWS = 16384
COLS = 16384
N_ROW = 8
N_COL = 16


def tile_lists(key, dense_count, capacity):
    devices = N_ROW * N_COL
    key_count, key_full, key_choose, key_rank = jax.random.split(key, 4)
    lowest = max(1, capacity // 2)
    counts = jax.random.randint(key_count, (devices,), lowest, capacity + 1)
    fullest = jax.random.randint(key_full, (), 0, devices)
    counts = jnp.where(jnp.arange(devices) == fullest, capacity, counts)
    choose_keys = jax.random.split(key_choose, devices)
    rank_keys = jax.random.split(key_rank, devices)
    chosen = jax.vmap(lambda sub_key: jax.random.permutation(sub_key, dense_count)[:capacity])(choose_keys)
    ranks = jax.vmap(lambda sub_key: jax.random.permutation(sub_key, capacity))(rank_keys)
    listed = jnp.where(ranks < counts[:, None], chosen, -1).astype(jnp.int32)
    return listed.reshape(N_ROW, N_COL, capacity).transpose(0, 2, 1).reshape(N_ROW * capacity, N_COL)


def draw_left_slots(key, part):
    key = jax.random.fold_in(key, 11)
    return tile_lists(key, RB_DEV * KB_DEV, CAP_A)


def draw_right_slots(key, part):
    key = jax.random.fold_in(key, 23)
    return tile_lists(key, KB_ROW * CB_DEV, CAP_B)


def levels(key, dims, pieces, least, largest):
    loudness, own = 1.0, jax.random.fold_in(key, 6)
    for dim, parts in pieces:
        draws = jnp.exp(jax.random.uniform(jax.random.fold_in(own, dim), (parts,), jnp.float32, least / len(pieces), largest / len(pieces)))
        loudness = loudness * jnp.repeat(draws, dims[dim] // parts).reshape([-1 if axis == dim else 1 for axis in range(len(dims))])
    return loudness


def setup_inputs(seed: int = 0) -> dict:
    key_list = jax.random.split(jax.random.key(seed), 5)
    left_tiles = jnp.clip(jnp.exp(math.log(0.049804688) - 4.6018058 * jax.random.uniform(key_list[0], (N_ROW * CAP_A, N_COL * TILE, TILE), jnp.float32) ** levels(key_list[0], (N_ROW * CAP_A, N_COL * TILE, TILE), ((0, 8), (1, 16)), -0.2, 0.2)), 0.00049972534, 0.049804688).astype(jnp.bfloat16)
    left_slots = draw_left_slots(jax.random.fold_in(key_list[4], 71), 0)
    right_tiles = jnp.clip(jnp.exp(math.log(0.049804688) - 4.6018058 * jax.random.uniform(key_list[2], (N_ROW * CAP_B, N_COL * TILE, TILE), jnp.float32) ** levels(key_list[2], (N_ROW * CAP_B, N_COL * TILE, TILE), ((0, 8), (1, 16)), -0.2, 0.2)), 0.00049972534, 0.049804688).astype(jnp.bfloat16)
    right_slots = draw_right_slots(jax.random.fold_in(key_list[4], 71), 0)
    return {"left_tiles": left_tiles, "left_slots": left_slots, "right_tiles": right_tiles, "right_slots": right_slots}


def place_left(left_tiles, left_slots):
    tile_set = left_tiles.reshape(N_ROW, CAP_A, N_COL, TILE, TILE).transpose(0, 2, 1, 3, 4)
    listed = left_slots.reshape(N_ROW, CAP_A, N_COL).transpose(0, 2, 1)
    row_dev = jnp.arange(N_ROW, dtype=jnp.int32)[:, None, None]
    col_dev = jnp.arange(N_COL, dtype=jnp.int32)[None, :, None]
    is_live = listed >= 0
    live_id = jnp.where(is_live, listed, 0)
    tile_row = jnp.where(is_live, row_dev * RB_DEV + live_id // KB_DEV, N_ROW * RB_DEV)
    tile_inner = col_dev * KB_DEV + live_id % KB_DEV
    dense = jnp.zeros((N_ROW * RB_DEV, KB_ALL, TILE, TILE), jnp.bfloat16)
    dense = dense.at[tile_row, tile_inner].set(tile_set, mode="drop")
    return dense.transpose(0, 2, 1, 3).reshape(ROWS, KB_ALL * TILE)


def place_right(right_tiles, right_slots):
    tile_set = right_tiles.reshape(N_ROW, CAP_B, N_COL, TILE, TILE).transpose(0, 2, 1, 3, 4)
    listed = right_slots.reshape(N_ROW, CAP_B, N_COL).transpose(0, 2, 1)
    row_dev = jnp.arange(N_ROW, dtype=jnp.int32)[:, None, None]
    col_dev = jnp.arange(N_COL, dtype=jnp.int32)[None, :, None]
    is_live = listed >= 0
    live_id = jnp.where(is_live, listed, 0)
    tile_inner = jnp.where(is_live, row_dev * KB_ROW + live_id // CB_DEV, KB_ALL)
    tile_col = col_dev * CB_DEV + live_id % CB_DEV
    dense = jnp.zeros((KB_ALL, N_COL * CB_DEV, TILE, TILE), jnp.bfloat16)
    dense = dense.at[tile_inner, tile_col].set(tile_set, mode="drop")
    return dense.transpose(0, 2, 1, 3).reshape(KB_ALL * TILE, COLS)


def reference(left_tiles, left_slots, right_tiles, right_slots):
    left = place_left(left_tiles, left_slots)
    right = place_right(right_tiles, right_slots)
    expanded = jnp.dot(left, right, preferred_element_type=jnp.float32)
    squared = expanded * expanded
    col_mean = jnp.sum(squared, axis=0) / ROWS
    return squared / (col_mean + 1e-6)
```

```python
import functools

import jax
import jax.numpy as jnp
from jax import lax
from jax.experimental import pallas as pl
from jax.experimental.pallas import tpu as pltpu
from jax.sharding import PartitionSpec as P

TILE = 256
RB_DEV = 8
CB_DEV = 4
CAP = 4
N_ROW = 8
N_COL = 16
SLAB = CAP * TILE
LANES = 128
EPSILON = 1e-06
MESH = pl.DeviceIdType.MESH
ANY = pl.BlockSpec(memory_space=pl.ANY)
VMEM = pl.BlockSpec(memory_space=pltpu.VMEM)
SMEM = pl.BlockSpec(memory_space=pltpu.SMEM)


class Factor:
    def __init__(self, out, own, place, device, send, recv, sibling):
        self.out, self.own, self.place, self.device = out, own, place, device
        self.send, self.recv, self.sibling = send, recv, sibling
        self.sent, self.count = [], 0

    def tile(self, slab, q):
        return self.out.at[self.place(*slab), pl.ds(q * TILE, TILE)]

    def start(self, slab, q, ring, pair):
        there = ((slab[0] - ring) % 4, (slab[1] - pair) % 2)
        source = self.own.at[pl.ds(q * TILE, TILE)] if slab == (0, 0) else self.tile(slab, q)
        copy = pltpu.make_async_remote_copy(
            src_ref=source,
            dst_ref=self.tile(slab, q),
            send_sem=self.send.at[self.count],
            recv_sem=self.recv.at[(there[0] + 4 * there[1]) * 4 + q],
            device_id=self.device(ring, pair),
            device_id_type=MESH,
        )
        copy.start()
        self.count += 1
        self.sent.append(copy)

    def arrived(self, slab, q):
        here = self.tile(slab, q)
        pltpu.make_async_copy(here, here, self.recv.at[(slab[0] + 4 * slab[1]) * 4 + q]).wait()
        if self.sibling is not None:
            self.sibling(self, slab, q)

    def begin(self, step):
        self.start((0, 0), (0, 3, 1, 2)[step], 0, 1)
        self.start((0, 0), step, 1, 0)
        self.start((0, 0), 3 - step, 3, 0)

    def events(self):
        def ring(pair, q, forward):
            def run():
                self.arrived((3, pair), q)
                if forward:
                    self.start((3, pair), q, 1, 0)
                self.arrived((1, pair), 3 - q)
                if forward:
                    self.start((1, pair), 3 - q, 3, 0)
            return run

        def across(q):
            def run():
                self.arrived((0, 1), q)
                self.start((0, 1), q, 1, 0)
                self.start((0, 1), q, 3, 0)
            return run

        def both(q, up, down):
            def run():
                self.arrived((3, 1), q)
                if up:
                    self.start((3, 1), q, 1, 0)
                self.arrived((1, 1), q)
                if down:
                    self.start((1, 1), q, 3, 0)
            return run

        def far(pair, q):
            def run():
                self.arrived((2, pair), q)
                self.arrived((2, pair), 3 - q)
            return run

        return [
            ring(0, 0, True), ring(0, 1, True), across(0), ring(0, 2, False), ring(0, 3, False),
            across(3), far(0, 0), far(0, 1), across(1), both(0, True, False), both(3, False, True),
            across(2), both(1, True, False), both(2, False, True), far(1, 0), far(1, 1),
        ]


def gather_kernel(left, right, left_slots, right_slots, left_all, right_all, left_ids, right_ids,
                  ids, left_send, left_recv, right_send, right_recv, sib_send, sib_recv,
                  idl_send, idl_recv, idr_send, idr_recv, own_sem):
    row, col = lax.axis_index("row"), lax.axis_index("col")
    y_hi, z = row // 4, lax.rem(row, 4)
    core, x, y_lo = lax.rem(col, 2), lax.rem(col // 2, 4), col // 8

    def left_place(ring, pair):
        return (lax.rem(y_lo + pair, 2) * 4 + lax.rem(x + ring, 4)) * 2 + core

    def right_place(ring, pair):
        return lax.rem(y_hi + pair, 2) * 4 + lax.rem(z + ring, 4)

    other = (row, col + 1 - 2 * core)

    barrier = pltpu.get_barrier_semaphore()
    for step in range(1, N_COL):
        pl.semaphore_signal(barrier, inc=1, device_id=(row, lax.rem(col + step, N_COL)), device_id_type=MESH)
    for step in range(1, N_ROW):
        pl.semaphore_signal(barrier, inc=1, device_id=(lax.rem(row + step, N_ROW), col), device_id_type=MESH)

    lane = lax.broadcasted_iota(jnp.int32, (1, LANES), 1)
    row_ids = jnp.full((1, LANES), -1, jnp.int32)
    for s in range(CAP):
        row_ids = jnp.where(lane == s, left_slots[s, 0], row_ids)
        row_ids = jnp.where(lane == CAP + s, right_slots[s, 0], row_ids)
    ids[...] = row_ids

    pl.semaphore_wait(barrier, N_COL + N_ROW - 2)

    shared = []

    def to_sibling(factor, slab, q):
        index = (slab[0] + 4 * slab[1]) * 4 + q
        part = factor.tile(slab, q)
        copy = pltpu.make_async_remote_copy(
            src_ref=factor.own.at[pl.ds(q * TILE, TILE)] if slab == (0, 0) else part,
            dst_ref=part,
            send_sem=sib_send.at[index],
            recv_sem=sib_recv.at[index],
            device_id=other,
            device_id_type=MESH,
        )
        copy.start()
        shared.append(copy)

    lf = Factor(left_all, left, left_place, lambda ring, pair: (row, left_place(ring, pair)), left_send, left_recv, to_sibling)
    rf = Factor(right_all, right, right_place, lambda ring, pair: (right_place(ring, pair), col), right_send, right_recv, None)

    for step in range(4):
        lf.begin(step)
        rf.begin(step)

    small = []
    for step in range(1, N_COL):
        copy = pltpu.make_async_remote_copy(
            src_ref=ids, dst_ref=left_ids.at[col], send_sem=idl_send.at[step], recv_sem=idl_recv.at[step],
            device_id=(row, lax.rem(col + step, N_COL)), device_id_type=MESH)
        copy.start()
        small.append(copy)
    for step in range(1, N_ROW):
        copy = pltpu.make_async_remote_copy(
            src_ref=ids, dst_ref=right_ids.at[row], send_sem=idr_send.at[step], recv_sem=idr_recv.at[step],
            device_id=(lax.rem(row + step, N_ROW), col), device_id_type=MESH)
        copy.start()
        small.append(copy)
    for q in range(CAP):
        to_sibling(lf, (0, 0), q)
    local = [
        pltpu.make_async_copy(left, left_all.at[col], own_sem.at[0]),
        pltpu.make_async_copy(right, right_all.at[row], own_sem.at[1]),
        pltpu.make_async_copy(ids, left_ids.at[col], own_sem.at[2]),
        pltpu.make_async_copy(ids, right_ids.at[row], own_sem.at[3]),
    ]
    for copy in local:
        copy.start()

    for left_event, right_event in zip(lf.events(), rf.events()):
        left_event()
        right_event()

    for copy in local:
        copy.wait()
    for index in range(8 * CAP):
        ring, pair, q = index // 4 % 4, index // 16, index % 4
        place = left_place(ring, pair) + 1 - 2 * core
        part = left_all.at[place, pl.ds(q * TILE, TILE)]
        pltpu.make_async_copy(part, part, sib_recv.at[index]).wait()
    for copy in small:
        copy.wait_recv()
    for copy in small + shared + lf.sent + rf.sent:
        copy.wait_send()


def gather(left, right, left_slots, right_slots):
    dma = pltpu.SemaphoreType.DMA
    return pl.pallas_call(
        gather_kernel,
        out_shape=[
            KEEP((N_COL, SLAB, TILE), jnp.bfloat16),
            KEEP((N_ROW, SLAB, TILE), jnp.bfloat16),
            jax.ShapeDtypeStruct((N_COL, 1, LANES), jnp.int32),
            jax.ShapeDtypeStruct((N_ROW, 1, LANES), jnp.int32),
        ],
        in_specs=[ANY, ANY, SMEM, SMEM],
        out_specs=[KEEP_SPEC, KEEP_SPEC, ANY, ANY],
        scratch_shapes=[
            pltpu.VMEM((1, LANES), jnp.int32),
            dma((28,)), dma((32,)), dma((28,)), dma((32,)), dma((32,)), dma((32,)),
            dma((N_COL,)), dma((N_COL,)), dma((N_ROW,)), dma((N_ROW,)), dma((4,)),
        ],
        compiler_params=pltpu.CompilerParams(collective_id=0, has_side_effects=True),
        name="gather_slabs",
    )(left, right, left_slots, right_slots)


def product_kernel(left_ids, right_ids, left_all, right_all, expanded, col_part):
    expanded[...] = jnp.zeros_like(expanded)

    def inner(k, _):
        for s in range(CAP):
            held = right_ids[k // 2, 0, CAP + s]

            @pl.when((held >= 0) & (held // CB_DEV == lax.rem(k, 2)))
            def _():
                j = lax.rem(held, CB_DEV)
                weights = right_all[k // 2, pl.ds(s * TILE, TILE)]
                for u in range(CAP):
                    i = left_ids[k, 0, u]

                    @pl.when(i >= 0)
                    def _():
                        part = jnp.dot(left_all[k, pl.ds(u * TILE, TILE)], weights, preferred_element_type=jnp.float32)
                        at = (pl.ds(pl.multiple_of(i * TILE, TILE), TILE), pl.ds(pl.multiple_of(j * TILE, TILE), TILE))
                        expanded[at] += part
        return 0

    lax.fori_loop(0, N_COL, inner, 0)

    def add(i, total):
        part = expanded[pl.ds(pl.multiple_of(i * 64, 64), 64)]
        return total + jnp.sum((part * part).reshape(8, 8, CB_DEV * TILE), axis=0)

    total = lax.fori_loop(0, RB_DEV * TILE // 64, add, jnp.zeros((8, CB_DEV * TILE), jnp.float32))
    col_part[...] = jnp.sum(total, axis=0, keepdims=True)


def product(left_ids, right_ids, left_all, right_all):
    return pl.pallas_call(
        product_kernel,
        out_shape=[
            KEEP((RB_DEV * TILE, CB_DEV * TILE), jnp.float32),
            jax.ShapeDtypeStruct((1, CB_DEV * TILE), jnp.float32),
        ],
        in_specs=[SMEM, SMEM, VMEM, VMEM],
        out_specs=[VMEM, VMEM],
        compiler_params=pltpu.CompilerParams(vmem_limit_bytes=24 * 2**20),
        name="tile_products",
    )(left_ids, right_ids, left_all, right_all)


def total_kernel(part, total, held, send, recv):
    row, col = lax.axis_index("row"), lax.axis_index("col")
    barrier = pltpu.get_barrier_semaphore()
    for step in range(1, N_ROW):
        pl.semaphore_signal(barrier, inc=1, device_id=(lax.rem(row + step, N_ROW), col), device_id_type=MESH)
    pl.semaphore_wait(barrier, N_ROW - 1)
    copies = []
    for step in range(1, N_ROW):
        copy = pltpu.make_async_remote_copy(
            src_ref=part, dst_ref=held.at[step], send_sem=send.at[step], recv_sem=recv.at[step],
            device_id=(lax.rem(row + step, N_ROW), col), device_id_type=MESH)
        copy.start()
        copies.append(copy)
    value = part[...]
    for step, copy in enumerate(copies):
        copy.wait_recv()
        value = value + held[step + 1]
    total[...] = value
    for copy in copies:
        copy.wait_send()


def column_total(part):
    dma = pltpu.SemaphoreType.DMA
    return pl.pallas_call(
        total_kernel,
        out_shape=jax.ShapeDtypeStruct(part.shape, part.dtype),
        in_specs=[VMEM],
        out_specs=VMEM,
        scratch_shapes=[pltpu.VMEM((N_ROW, *part.shape), part.dtype), dma((N_ROW,)), dma((N_ROW,))],
        compiler_params=pltpu.CompilerParams(collective_id=1, has_side_effects=True),
        name="column_total",
    )(part)


def scale_kernel(total, expanded, out):
    factor = 1.0 / (total[...] / (RB_DEV * TILE * N_ROW) + EPSILON)
    value = expanded[...]
    out[...] = value * value * factor


def scale(total, expanded):
    rows, cols = expanded.shape
    step = 256
    return pl.pallas_call(
        scale_kernel,
        grid=(rows // step,),
        out_shape=jax.ShapeDtypeStruct(expanded.shape, jnp.float32),
        in_specs=[pl.BlockSpec((1, cols), lambda i: (0, 0)), pl.BlockSpec((step, cols), lambda i: (i, 0))],
        out_specs=pl.BlockSpec((step, cols), lambda i: (i, 0)),
        name="scale_columns",
    )(total, expanded)


KEEP = jax.ShapeDtypeStruct
KEEP_SPEC = ANY


def body(left_tiles, left_slots, right_tiles, right_slots):
    left = left_tiles.reshape(SLAB, TILE)
    right = right_tiles.reshape(SLAB, TILE)
    left_all, right_all, left_ids, right_ids = gather(left, right, left_slots, right_slots)
    expanded, col_part = product(left_ids, right_ids, left_all, right_all)
    return scale(column_total(col_part), expanded)


def solution(mesh):
    placed = (P("row", "col", None), P("row", "col"), P("row", "col", None), P("row", "col"))
    return jax.shard_map(
        body, mesh=mesh, in_specs=placed, out_specs=P("row", "col"), check_vma=False
    )
```

```python
import functools

import jax
import jax.numpy as jnp
from jax import lax
from jax.experimental import pallas as pl
from jax.experimental.pallas import tpu as pltpu
from jax.sharding import PartitionSpec as P

TILE = 256
RB_DEV = 8
CB_DEV = 4
CAP = 4
N_ROW = 8
N_COL = 16
SLAB = CAP * TILE
LANES = 128
EPSILON = 1e-06
MESH = pl.DeviceIdType.MESH
ANY = pl.BlockSpec(memory_space=pl.ANY)
VMEM = pl.BlockSpec(memory_space=pltpu.VMEM)
SMEM = pl.BlockSpec(memory_space=pltpu.SMEM)
HBM = pl.BlockSpec(memory_space=pltpu.HBM)


class Factor:
    UP = [((0, 0), q) for q in (0, 1, 2, 3)] + [((3, 0), 0), ((3, 0), 2)] + [((0, 1), q) for q in (0, 1, 2, 3)] + [((3, 1), 0), ((3, 1), 2)]
    DOWN = [((0, 0), q) for q in (1, 0, 3, 2)] + [((1, 0), 1), ((1, 0), 3)] + [((0, 1), q) for q in (1, 0, 2, 3)] + [((1, 1), 1), ((1, 1), 3)]
    TICKS = len(UP)
    WINDOW = 2

    def __init__(self, out, own, place, device, send, recv, sibling):
        self.out, self.own, self.place, self.device = out, own, place, device
        self.send, self.recv, self.sibling = send, recv, sibling
        self.count, self.here = 0, set()
        self.lines = {"up": [], "down": [], "pair": []}

    def tile(self, slab, q):
        return self.out.at[self.place(*slab), pl.ds(q * TILE, TILE)]

    def start(self, line, slab, q, ring, pair):
        sent = self.lines[line]
        if len(sent) >= self.WINDOW:
            sent[-self.WINDOW].wait_send()
        if slab != (0, 0):
            self.arrived(slab, q)
        there = ((slab[0] - ring) % 4, (slab[1] - pair) % 2)
        source = self.own.at[pl.ds(q * TILE, TILE)] if slab == (0, 0) else self.tile(slab, q)
        copy = pltpu.make_async_remote_copy(
            src_ref=source,
            dst_ref=self.tile(slab, q),
            send_sem=self.send.at[self.count],
            recv_sem=self.recv.at[(there[0] + 4 * there[1]) * 4 + q],
            device_id=self.device(ring, pair),
            device_id_type=MESH,
        )
        copy.start()
        self.count += 1
        sent.append(copy)

    def arrived(self, slab, q):
        if (slab, q) in self.here:
            return
        self.here.add((slab, q))
        here = self.tile(slab, q)
        pltpu.make_async_copy(here, here, self.recv.at[(slab[0] + 4 * slab[1]) * 4 + q]).wait()
        if self.sibling is not None:
            self.sibling(self, slab, q)

    def tick(self, t):
        if t % 2 == 0 and t // 2 < CAP:
            self.start("pair", (0, 0), t // 2, 0, 1)
        if t < self.TICKS:
            self.start("up", *self.UP[t], 1, 0)
            self.start("down", *self.DOWN[t], 3, 0)
        if 2 <= t < self.TICKS + 2:
            (ring, pair), q = self.UP[t - 2]
            self.arrived(((ring + 3) % 4, pair), q)
            (ring, pair), q = self.DOWN[t - 2]
            self.arrived(((ring + 1) % 4, pair), q)

    def finish(self):
        for line in self.lines.values():
            for copy in line[-self.WINDOW:]:
                copy.wait_send()


def gather_kernel(left, right, left_slots, right_slots, left_all, right_all, left_ids, right_ids,
                  ids, slots, left_send, left_recv, right_send, right_recv, sib_send, sib_recv,
                  idl_send, idl_recv, idr_send, idr_recv, own_sem):
    row, col = lax.axis_index("row"), lax.axis_index("col")
    y_hi, z = row // 4, lax.rem(row, 4)
    core, x, y_lo = lax.rem(col, 2), lax.rem(col // 2, 4), col // 8

    def left_place(ring, pair):
        return (lax.rem(y_lo + pair, 2) * 4 + lax.rem(x + ring, 4)) * 2 + core

    def right_place(ring, pair):
        return lax.rem(y_hi + pair, 2) * 4 + lax.rem(z + ring, 4)

    other = (row, col + 1 - 2 * core)

    fetch = [
        pltpu.make_async_copy(left_slots, slots.at[pl.ds(0, 1)], own_sem.at[4]),
        pltpu.make_async_copy(right_slots, slots.at[pl.ds(1, 1)], own_sem.at[5]),
    ]
    for copy in fetch:
        copy.start()
    barrier = pltpu.get_barrier_semaphore()
    for step in range(1, N_COL):
        pl.semaphore_signal(barrier, inc=1, device_id=(row, lax.rem(col + step, N_COL)), device_id_type=MESH)
    for step in range(1, N_ROW):
        pl.semaphore_signal(barrier, inc=1, device_id=(lax.rem(row + step, N_ROW), col), device_id_type=MESH)

    lane = lax.broadcasted_iota(jnp.int32, (1, LANES), 1)
    for copy in fetch:
        copy.wait()
    row_ids = jnp.full((1, LANES), -1, jnp.int32)
    for s in range(CAP):
        row_ids = jnp.where(lane == s, slots[0, s], row_ids)
        row_ids = jnp.where(lane == CAP + s, slots[1, s], row_ids)
    ids[...] = row_ids

    pl.semaphore_wait(barrier, N_COL + N_ROW - 2)

    shared = []

    def to_sibling(factor, slab, q):
        index = (slab[0] + 4 * slab[1]) * 4 + q
        part = factor.tile(slab, q)
        copy = pltpu.make_async_remote_copy(
            src_ref=factor.own.at[pl.ds(q * TILE, TILE)] if slab == (0, 0) else part,
            dst_ref=part,
            send_sem=sib_send.at[index],
            recv_sem=sib_recv.at[index],
            device_id=other,
            device_id_type=MESH,
        )
        copy.start()
        shared.append(copy)

    lf = Factor(left_all, left, left_place, lambda ring, pair: (row, left_place(ring, pair)), left_send, left_recv, to_sibling)
    rf = Factor(right_all, right, right_place, lambda ring, pair: (right_place(ring, pair), col), right_send, right_recv, None)

    lf.tick(0)
    rf.tick(0)
    lf.tick(1)
    rf.tick(1)

    small = []
    for step in range(1, N_COL):
        copy = pltpu.make_async_remote_copy(
            src_ref=ids, dst_ref=left_ids.at[col], send_sem=idl_send.at[step], recv_sem=idl_recv.at[step],
            device_id=(row, lax.rem(col + step, N_COL)), device_id_type=MESH)
        copy.start()
        small.append(copy)
    for step in range(1, N_ROW):
        copy = pltpu.make_async_remote_copy(
            src_ref=ids, dst_ref=right_ids.at[row], send_sem=idr_send.at[step], recv_sem=idr_recv.at[step],
            device_id=(lax.rem(row + step, N_ROW), col), device_id_type=MESH)
        copy.start()
        small.append(copy)
    for q in range(CAP):
        to_sibling(lf, (0, 0), q)
    local = [
        pltpu.make_async_copy(left, left_all.at[col], own_sem.at[0]),
        pltpu.make_async_copy(right, right_all.at[row], own_sem.at[1]),
        pltpu.make_async_copy(ids, left_ids.at[col], own_sem.at[2]),
        pltpu.make_async_copy(ids, right_ids.at[row], own_sem.at[3]),
    ]
    for copy in local:
        copy.start()

    for t in range(2, Factor.TICKS + 2):
        lf.tick(t)
        rf.tick(t)

    for copy in local:
        copy.wait()
    for index in range(8 * CAP):
        ring, pair, q = index // 4 % 4, index // 16, index % 4
        place = left_place(ring, pair) + 1 - 2 * core
        part = left_all.at[place, pl.ds(q * TILE, TILE)]
        pltpu.make_async_copy(part, part, sib_recv.at[index]).wait()
    for copy in small:
        copy.wait_recv()
    for copy in small + shared:
        copy.wait_send()
    lf.finish()
    rf.finish()


def gather(left, right, left_slots, right_slots):
    dma = pltpu.SemaphoreType.DMA
    operands = [pltpu.with_memory_space_constraint(x, pltpu.HBM) for x in (left, right, left_slots, right_slots)]
    return pl.pallas_call(
        gather_kernel,
        out_shape=[
            KEEP((N_COL, SLAB, TILE), jnp.bfloat16),
            KEEP((N_ROW, SLAB, TILE), jnp.bfloat16),
            jax.ShapeDtypeStruct((N_COL, 1, LANES), jnp.int32),
            jax.ShapeDtypeStruct((N_ROW, 1, LANES), jnp.int32),
        ],
        in_specs=[HBM, HBM, HBM, HBM],
        out_specs=[KEEP_SPEC, KEEP_SPEC, ANY, ANY],
        scratch_shapes=[
            pltpu.VMEM((1, LANES), jnp.int32),
            pltpu.SMEM((2, CAP), jnp.int32),
            dma((28,)), dma((32,)), dma((28,)), dma((32,)), dma((32,)), dma((32,)),
            dma((N_COL,)), dma((N_COL,)), dma((N_ROW,)), dma((N_ROW,)), dma((6,)),
        ],
        compiler_params=pltpu.CompilerParams(collective_id=0, has_side_effects=True, vmem_limit_bytes=2**20),
        name="gather_slabs",
    )(*operands)


def product_kernel(left_ids, right_ids, left_all, right_all, expanded, col_part):
    expanded[...] = jnp.zeros_like(expanded)

    def inner(n, _):
        q, s = n // CAP, lax.rem(n, CAP)
        held = right_ids[q, 0, CAP + s]

        @pl.when(held >= 0)
        def _():
            k, j = 2 * q + held // CB_DEV, lax.rem(held, CB_DEV)
            weights = right_all[q, pl.ds(pl.multiple_of(s * TILE, TILE), TILE)]
            part = jnp.dot(left_all[k], weights, preferred_element_type=jnp.float32)
            for u in range(CAP):
                i = left_ids[k, 0, u]
                i = jnp.where(i < 0, RB_DEV, i)
                at = (pl.ds(pl.multiple_of(i * TILE, TILE), TILE), pl.ds(pl.multiple_of(j * TILE, TILE), TILE))
                expanded[at] += part[u * TILE : (u + 1) * TILE]
        return 0

    lax.fori_loop(0, N_ROW * CAP, inner, 0)

    def add(i, total):
        part = expanded[pl.ds(pl.multiple_of(i * 64, 64), 64)]
        return total + jnp.sum((part * part).reshape(8, 8, CB_DEV * TILE), axis=0)

    total = lax.fori_loop(0, RB_DEV * TILE // 64, add, jnp.zeros((8, CB_DEV * TILE), jnp.float32))
    col_part[...] = jnp.sum(total, axis=0, keepdims=True)


def product(left_ids, right_ids, left_all, right_all):
    return pl.pallas_call(
        product_kernel,
        out_shape=[
            KEEP(((RB_DEV + 1) * TILE, CB_DEV * TILE), jnp.float32),
            jax.ShapeDtypeStruct((1, CB_DEV * TILE), jnp.float32),
        ],
        in_specs=[SMEM, SMEM, VMEM, VMEM],
        out_specs=[VMEM, VMEM],
        compiler_params=pltpu.CompilerParams(vmem_limit_bytes=4 * 2**20),
        name="tile_products",
    )(left_ids, right_ids, left_all, right_all)


def total_kernel(part, total, held, send, recv):
    row, col = lax.axis_index("row"), lax.axis_index("col")
    barrier = pltpu.get_barrier_semaphore()
    for step in range(1, N_ROW):
        pl.semaphore_signal(barrier, inc=1, device_id=(lax.rem(row + step, N_ROW), col), device_id_type=MESH)
    pl.semaphore_wait(barrier, N_ROW - 1)
    copies = []
    for step in range(1, N_ROW):
        copy = pltpu.make_async_remote_copy(
            src_ref=part, dst_ref=held.at[step], send_sem=send.at[step], recv_sem=recv.at[step],
            device_id=(lax.rem(row + step, N_ROW), col), device_id_type=MESH)
        copy.start()
        copies.append(copy)
    value = part[...]
    for step, copy in enumerate(copies):
        copy.wait_recv()
        value = value + held[step + 1]
    total[...] = value
    for copy in copies:
        copy.wait_send()


def column_total(part):
    dma = pltpu.SemaphoreType.DMA
    return pl.pallas_call(
        total_kernel,
        out_shape=jax.ShapeDtypeStruct(part.shape, part.dtype),
        in_specs=[VMEM],
        out_specs=VMEM,
        scratch_shapes=[pltpu.VMEM((N_ROW, *part.shape), part.dtype), dma((N_ROW,)), dma((N_ROW,))],
        compiler_params=pltpu.CompilerParams(collective_id=1, has_side_effects=True, vmem_limit_bytes=2**20),
        name="column_total",
    )(part)


SCALE_ROWS = 128
SCALE_SLOTS = 4


def scale_kernel(total, expanded, out, scaled, sems):
    factor = 1.0 / (total[...] / (RB_DEV * TILE * N_ROW) + EPSILON)
    copies = []
    for n in range(RB_DEV * TILE // SCALE_ROWS):
        slot = n % SCALE_SLOTS
        if n >= SCALE_SLOTS:
            copies[n - SCALE_SLOTS].wait()
        rows = pl.ds(n * SCALE_ROWS, SCALE_ROWS)
        value = expanded[rows]
        scaled[slot] = value * value * factor
        copy = pltpu.make_async_copy(scaled.at[slot], out.at[rows], sems.at[slot])
        copy.start()
        copies.append(copy)
    for copy in copies[-SCALE_SLOTS:]:
        copy.wait()


def scale(total, expanded):
    cols = expanded.shape[1]
    return pl.pallas_call(
        scale_kernel,
        out_shape=jax.ShapeDtypeStruct((RB_DEV * TILE, cols), jnp.float32),
        in_specs=[VMEM, VMEM],
        out_specs=ANY,
        scratch_shapes=[pltpu.VMEM((SCALE_SLOTS, SCALE_ROWS, cols), jnp.float32), pltpu.SemaphoreType.DMA((SCALE_SLOTS,))],
        compiler_params=pltpu.CompilerParams(vmem_limit_bytes=4 * 2**20),
        name="scale_columns",
    )(total, expanded)


KEEP = jax.ShapeDtypeStruct
KEEP_SPEC = ANY


def body(left_tiles, left_slots, right_tiles, right_slots):
    left = left_tiles.reshape(SLAB, TILE)
    right = right_tiles.reshape(SLAB, TILE)
    left_all, right_all, left_ids, right_ids = gather(
        left, right, left_slots.reshape(1, CAP), right_slots.reshape(1, CAP)
    )
    expanded, col_part = product(left_ids, right_ids, left_all, right_all)
    return scale(column_total(col_part), expanded)


def solution(mesh):
    placed = (P("row", "col", None), P("row", "col"), P("row", "col", None), P("row", "col"))
    return jax.shard_map(
        body, mesh=mesh, in_specs=placed, out_specs=P("row", "col"), check_vma=False
    )
```

```python
import functools

import jax
import jax.numpy as jnp
from jax import lax
from jax.experimental import pallas as pl
from jax.experimental.pallas import tpu as pltpu
from jax.sharding import PartitionSpec as P

TILE = 256
RB_DEV = 8
CB_DEV = 4
CAP = 4
N_ROW = 8
N_COL = 16
SLAB = CAP * TILE
LANES = 128
EPSILON = 1e-06
MESH = pl.DeviceIdType.MESH
ANY = pl.BlockSpec(memory_space=pl.ANY)
VMEM = pl.BlockSpec(memory_space=pltpu.VMEM)
SMEM = pl.BlockSpec(memory_space=pltpu.SMEM)


IDS_ALONG = [("pair", (0, 0)), ("up", (0, 0)), ("up", (3, 0)), ("up", (0, 1)), ("up", (3, 1)), ("down", (0, 0)), ("down", (0, 1))]


class Factor:
    UP = [((0, 0), q) for q in (0, 1, 2, 3)] + [((3, 0), 0), ((3, 0), 2)] + [((0, 1), q) for q in (0, 1, 2, 3)] + [((3, 1), 0), ((3, 1), 2)]
    DOWN = [((0, 0), q) for q in (1, 0, 3, 2)] + [((1, 0), 1), ((1, 0), 3)] + [((0, 1), q) for q in (1, 0, 2, 3)] + [((1, 1), 1), ((1, 1), 3)]
    TICKS = len(UP)
    WINDOW = 2

    def __init__(self, out, own, place, device, send, recv, sibling, ids_out, ids_own, ids_place, ids_send, ids_recv):
        self.out, self.own, self.place, self.device = out, own, place, device
        self.send, self.recv, self.sibling = send, recv, sibling
        self.ids_out, self.ids_own, self.ids_place, self.ids_send, self.ids_recv = ids_out, ids_own, ids_place, ids_send, ids_recv
        self.count, self.here, self.ids_here, self.ids_sent = 0, set(), set(), []
        self.lines_with_ids = {(line, slab) for line, slab in IDS_ALONG}
        self.lines = {"up": [], "down": [], "pair": []}

    def tile(self, slab, q):
        return self.out.at[self.place(*slab), pl.ds(q * TILE, TILE)]

    def start(self, line, slab, q, ring, pair):
        sent = self.lines[line]
        if len(sent) >= self.WINDOW:
            sent[-self.WINDOW].wait_send()
        if slab != (0, 0):
            self.arrived(slab, q)
        there = ((slab[0] - ring) % 4, (slab[1] - pair) % 2)
        source = self.own.at[pl.ds(q * TILE, TILE)] if slab == (0, 0) else self.tile(slab, q)
        copy = pltpu.make_async_remote_copy(
            src_ref=source,
            dst_ref=self.tile(slab, q),
            send_sem=self.send.at[self.count],
            recv_sem=self.recv.at[(there[0] + 4 * there[1]) * 4 + q],
            device_id=self.device(ring, pair),
            device_id_type=MESH,
        )
        copy.start()
        self.count += 1
        sent.append(copy)
        if (line, slab) in self.lines_with_ids:
            self.lines_with_ids.remove((line, slab))
            self.start_ids(slab, there, ring, pair)

    def start_ids(self, slab, there, ring, pair):
        if slab != (0, 0):
            self.ids_arrived(slab)
        copy = pltpu.make_async_remote_copy(
            src_ref=self.ids_own if slab == (0, 0) else self.ids_out.at[self.ids_place(*slab)],
            dst_ref=self.ids_out.at[self.ids_place(*slab)],
            send_sem=self.ids_send.at[len(self.ids_sent)],
            recv_sem=self.ids_recv.at[there[0] + 4 * there[1]],
            device_id=self.device(ring, pair),
            device_id_type=MESH,
        )
        copy.start()
        self.ids_sent.append(copy)

    def ids_arrived(self, slab):
        if slab not in self.ids_here:
            self.ids_here.add(slab)
            here = self.ids_out.at[self.ids_place(*slab)]
            pltpu.make_async_copy(here, here, self.ids_recv.at[slab[0] + 4 * slab[1]]).wait()

    def arrived(self, slab, q):
        if (slab, q) in self.here:
            return
        self.here.add((slab, q))
        here = self.tile(slab, q)
        pltpu.make_async_copy(here, here, self.recv.at[(slab[0] + 4 * slab[1]) * 4 + q]).wait()
        if self.sibling is not None:
            self.sibling(self, slab, q)

    def tick(self, t):
        if t % 2 == 0 and t // 2 < CAP:
            self.start("pair", (0, 0), t // 2, 0, 1)
        if t < self.TICKS:
            self.start("up", *self.UP[t], 1, 0)
            self.start("down", *self.DOWN[t], 3, 0)
        if 2 <= t < self.TICKS + 2:
            (ring, pair), q = self.UP[t - 2]
            self.arrived(((ring + 3) % 4, pair), q)
            (ring, pair), q = self.DOWN[t - 2]
            self.arrived(((ring + 1) % 4, pair), q)

    def finish(self):
        for line in self.lines.values():
            for copy in line[-self.WINDOW:]:
                copy.wait_send()
        for copy in self.ids_sent:
            copy.wait_send()


def gather_kernel(left, right, left_slots, right_slots, left_all, right_all, left_ids, right_ids,
                  ids, slots, left_send, left_recv, right_send, right_recv, sib_send, sib_recv,
                  idl_send, idl_recv, idr_send, idr_recv, ids_sib, own_sem):
    row, col = lax.axis_index("row"), lax.axis_index("col")
    y_hi, z = row // 4, lax.rem(row, 4)
    core, x, y_lo = lax.rem(col, 2), lax.rem(col // 2, 4), col // 8

    def left_place(ring, pair):
        return (lax.rem(y_lo + pair, 2) * 4 + lax.rem(x + ring, 4)) * 2 + core

    def right_place(ring, pair):
        return lax.rem(y_hi + pair, 2) * 4 + lax.rem(z + ring, 4)

    other = (row, col + 1 - 2 * core)

    fetch = [
        pltpu.make_async_copy(left_slots, slots.at[pl.ds(0, 1)], own_sem.at[4]),
        pltpu.make_async_copy(right_slots, slots.at[pl.ds(1, 1)], own_sem.at[5]),
    ]
    for copy in fetch:
        copy.start()
    barrier = pltpu.get_barrier_semaphore()
    for peer in (
        (row, left_place(1, 0)), (row, left_place(3, 0)), (row, left_place(0, 1)), other,
        (right_place(1, 0), col), (right_place(3, 0), col), (right_place(0, 1), col),
    ):
        pl.semaphore_signal(barrier, inc=1, device_id=peer, device_id_type=MESH)

    lane = lax.broadcasted_iota(jnp.int32, (1, LANES), 1)
    for copy in fetch:
        copy.wait()
    row_ids = jnp.full((1, LANES), -1, jnp.int32)
    for s in range(CAP):
        row_ids = jnp.where(lane == s, slots[0, s], row_ids)
        row_ids = jnp.where(lane == CAP + s, slots[1, s], row_ids)
    ids[...] = row_ids

    pl.semaphore_wait(barrier, 7)

    shared = []

    def to_sibling(factor, slab, q):
        index = (slab[0] + 4 * slab[1]) * 4 + q
        part = factor.tile(slab, q)
        copy = pltpu.make_async_remote_copy(
            src_ref=factor.own.at[pl.ds(q * TILE, TILE)] if slab == (0, 0) else part,
            dst_ref=part,
            send_sem=sib_send.at[index],
            recv_sem=sib_recv.at[index],
            device_id=other,
            device_id_type=MESH,
        )
        copy.start()
        shared.append(copy)

    def left_ids_place(ring, pair):
        return core * N_ROW + left_place(ring, pair) // 2

    lf = Factor(
        left_all, left, left_place, lambda ring, pair: (row, left_place(ring, pair)), left_send, left_recv, to_sibling,
        left_ids, ids, left_ids_place, idl_send, idl_recv,
    )
    rf = Factor(
        right_all, right, right_place, lambda ring, pair: (right_place(ring, pair), col), right_send, right_recv, None,
        right_ids, ids, right_place, idr_send, idr_recv,
    )

    lf.tick(0)
    rf.tick(0)
    lf.tick(1)
    rf.tick(1)

    for q in range(CAP):
        to_sibling(lf, (0, 0), q)
    local = [
        pltpu.make_async_copy(left, left_all.at[col], own_sem.at[0]),
        pltpu.make_async_copy(right, right_all.at[row], own_sem.at[1]),
        pltpu.make_async_copy(ids, left_ids.at[left_ids_place(0, 0)], own_sem.at[2]),
        pltpu.make_async_copy(ids, right_ids.at[row], own_sem.at[3]),
    ]
    for copy in local:
        copy.start()

    for t in range(2, Factor.TICKS + 2):
        lf.tick(t)
        rf.tick(t)

    for copy in local:
        copy.wait()
    for slab in [(ring, pair) for pair in range(2) for ring in range(4)][1:]:
        lf.ids_arrived(slab)
        rf.ids_arrived(slab)
    block = left_ids.at[pl.ds(core * N_ROW, N_ROW)]
    copy = pltpu.make_async_remote_copy(
        src_ref=block, dst_ref=block, send_sem=ids_sib.at[0], recv_sem=ids_sib.at[1], device_id=other, device_id_type=MESH)
    copy.start()
    shared.append(copy)
    for index in range(8 * CAP):
        ring, pair, q = index // 4 % 4, index // 16, index % 4
        place = left_place(ring, pair) + 1 - 2 * core
        part = left_all.at[place, pl.ds(q * TILE, TILE)]
        pltpu.make_async_copy(part, part, sib_recv.at[index]).wait()
    theirs = left_ids.at[pl.ds((1 - core) * N_ROW, N_ROW)]
    pltpu.make_async_copy(theirs, theirs, ids_sib.at[1]).wait()
    for copy in shared:
        copy.wait_send()
    lf.finish()
    rf.finish()


def gather(left, right, left_slots, right_slots):
    dma = pltpu.SemaphoreType.DMA
    operands = [pltpu.with_memory_space_constraint(x, pltpu.HBM) for x in (left, right, left_slots, right_slots)]
    return pl.pallas_call(
        gather_kernel,
        out_shape=[
            jax.ShapeDtypeStruct((N_COL, SLAB, TILE), jnp.bfloat16),
            jax.ShapeDtypeStruct((N_ROW, SLAB, TILE), jnp.bfloat16),
            jax.ShapeDtypeStruct((N_COL, 1, LANES), jnp.int32),
            jax.ShapeDtypeStruct((N_ROW, 1, LANES), jnp.int32),
        ],
        in_specs=[ANY, ANY, ANY, ANY],
        out_specs=[ANY, ANY, ANY, ANY],
        scratch_shapes=[
            pltpu.VMEM((1, LANES), jnp.int32),
            pltpu.SMEM((2, CAP), jnp.int32),
            dma((28,)), dma((32,)), dma((28,)), dma((32,)), dma((32,)), dma((32,)),
            dma((7,)), dma((8,)), dma((7,)), dma((8,)), dma((2,)), dma((6,)),
        ],
        compiler_params=pltpu.CompilerParams(collective_id=0, has_side_effects=True, vmem_limit_bytes=2**20),
        name="gather_slabs",
    )(*operands)


PER_STEP = 8


def product_kernel(left_ids, right_ids, left_all, right_all, expanded):
    expanded[...] = jnp.zeros_like(expanded)

    def inner(n, _):
        work = []
        for w in range(PER_STEP):
            q, s = n * (PER_STEP // CAP) + w // CAP, w % CAP
            held = right_ids[q, 0, CAP + s]
            kept = held >= 0
            held = jnp.where(kept, held, 0)
            parity = held // CB_DEV
            rows = []
            for u in range(CAP):
                i = left_ids[parity * N_ROW + q, 0, u]
                rows.append(jnp.where(kept & (i >= 0), i, RB_DEV))
            work.append((q, s, 2 * q + parity, lax.rem(held, CB_DEV), rows))
        for q, s, k, j, rows in work:
            weights = right_all[q, s * TILE : (s + 1) * TILE]
            for u, i in enumerate(rows):
                at = (pl.ds(pl.multiple_of(i * TILE, TILE), TILE), pl.ds(pl.multiple_of(j * TILE, TILE), TILE))
                expanded[at] += jnp.dot(
                    left_all[k, u * TILE : (u + 1) * TILE], weights, preferred_element_type=jnp.float32
                )
        return 0

    lax.fori_loop(0, N_ROW * CAP // PER_STEP, inner, 0)


def product(left_ids, right_ids, left_all, right_all):
    return pl.pallas_call(
        product_kernel,
        out_shape=jax.ShapeDtypeStruct(((RB_DEV + 1) * TILE, CB_DEV * TILE), jnp.float32),
        in_specs=[SMEM, SMEM, VMEM, VMEM],
        out_specs=VMEM,
        compiler_params=pltpu.CompilerParams(vmem_limit_bytes=4 * 2**20),
        name="tile_products",
    )(left_ids, right_ids, left_all, right_all)


def total_kernel(expanded, total, part, held, send, recv):
    row, col = lax.axis_index("row"), lax.axis_index("col")
    peers = [(lax.rem(row + step, N_ROW), col) for step in range(1, N_ROW)]
    barrier = pltpu.get_barrier_semaphore()
    for peer in peers:
        pl.semaphore_signal(barrier, inc=1, device_id=peer, device_id_type=MESH)

    def add(i, sums):
        rows = expanded[pl.ds(pl.multiple_of(i * 64, 64), 64)]
        return sums + jnp.sum((rows * rows).reshape(8, 8, CB_DEV * TILE), axis=0)

    sums = lax.fori_loop(0, RB_DEV * TILE // 64, add, jnp.zeros((8, CB_DEV * TILE), jnp.float32))
    part[...] = jnp.sum(sums, axis=0, keepdims=True)
    pl.semaphore_wait(barrier, N_ROW - 1)
    copies = []
    for n, peer in enumerate(peers):
        copy = pltpu.make_async_remote_copy(
            src_ref=part, dst_ref=held.at[n], send_sem=send.at[n], recv_sem=recv.at[n],
            device_id=peer, device_id_type=MESH)
        copy.start()
        copies.append(copy)
    value = part[...]
    for n, copy in enumerate(copies):
        copy.wait_recv()
        value = value + held[n]
    total[...] = value
    for copy in copies:
        copy.wait_send()


def column_total(expanded):
    dma = pltpu.SemaphoreType.DMA
    shape = (1, CB_DEV * TILE)
    return pl.pallas_call(
        total_kernel,
        out_shape=jax.ShapeDtypeStruct(shape, jnp.float32),
        in_specs=[VMEM],
        out_specs=VMEM,
        scratch_shapes=[
            pltpu.VMEM(shape, jnp.float32), pltpu.VMEM((N_ROW - 1, *shape), jnp.float32), dma((N_ROW - 1,)), dma((N_ROW - 1,)),
        ],
        compiler_params=pltpu.CompilerParams(collective_id=1, has_side_effects=True, vmem_limit_bytes=2**20),
        name="column_total",
    )(expanded)


SCALE_ROWS = 128
SCALE_SLOTS = 4


def scale_kernel(total, expanded, out, scaled, sems):
    factor = 1.0 / (total[...] / (RB_DEV * TILE * N_ROW) + EPSILON)
    copies = []
    for n in range(RB_DEV * TILE // SCALE_ROWS):
        slot = n % SCALE_SLOTS
        if n >= SCALE_SLOTS:
            copies[n - SCALE_SLOTS].wait()
        rows = pl.ds(n * SCALE_ROWS, SCALE_ROWS)
        value = expanded[rows]
        scaled[slot] = value * value * factor
        copy = pltpu.make_async_copy(scaled.at[slot], out.at[rows], sems.at[slot])
        copy.start()
        copies.append(copy)
    for copy in copies[-SCALE_SLOTS:]:
        copy.wait()


def scale(total, expanded):
    cols = expanded.shape[1]
    return pl.pallas_call(
        scale_kernel,
        out_shape=jax.ShapeDtypeStruct((RB_DEV * TILE, cols), jnp.float32),
        in_specs=[VMEM, VMEM],
        out_specs=ANY,
        scratch_shapes=[pltpu.VMEM((SCALE_SLOTS, SCALE_ROWS, cols), jnp.float32), pltpu.SemaphoreType.DMA((SCALE_SLOTS,))],
        compiler_params=pltpu.CompilerParams(vmem_limit_bytes=4 * 2**20),
        name="scale_columns",
    )(total, expanded)


def body(left_tiles, left_slots, right_tiles, right_slots):
    left = left_tiles.reshape(SLAB, TILE)
    right = right_tiles.reshape(SLAB, TILE)
    left_all, right_all, left_ids, right_ids = gather(
        left, right, left_slots.reshape(1, CAP), right_slots.reshape(1, CAP)
    )
    expanded = product(left_ids, right_ids, left_all, right_all)
    return scale(column_total(expanded), expanded)


def solution(mesh):
    placed = (P("row", "col", None), P("row", "col"), P("row", "col", None), P("row", "col"))
    return jax.shard_map(
        body, mesh=mesh, in_specs=placed, out_specs=P("row", "col"), check_vma=False
    )
```

```python
import functools

import jax
import jax.numpy as jnp
from jax import lax
from jax.experimental import pallas as pl
from jax.experimental.pallas import tpu as pltpu
from jax.sharding import PartitionSpec as P

TILE = 256
RB_DEV = 8
CB_DEV = 4
CAP = 4
N_ROW = 8
N_COL = 16
SLAB = CAP * TILE
LANES = 128
EPSILON = 1e-06
MESH = pl.DeviceIdType.MESH
ANY = pl.BlockSpec(memory_space=pl.ANY)
VMEM = pl.BlockSpec(memory_space=pltpu.VMEM)
SMEM = pl.BlockSpec(memory_space=pltpu.SMEM)


IDS_ALONG = [("pair", (0, 0)), ("up", (0, 0)), ("up", (3, 0)), ("up", (0, 1)), ("down", (0, 0)), ("down", (0, 1))]
PIECES = [(0, TILE), (TILE, TILE), (2 * TILE, TILE), (3 * TILE, TILE), (2 * TILE, TILE // 2), (2 * TILE + TILE // 2, TILE // 2)]


class Factor:
    WINDOW = 2

    def __init__(self, out, own, place, device, send, recv, sibling, ids_out, ids_own, ids_place, ids_send, ids_recv, across):
        self.across = across
        halves = 2 not in across
        self.UP = [((0, 0), q) for q in (0, 1, 2, 3)] + [((3, 0), 0), ((3, 0), 2)] + [((0, 1), q) for q in (0, 1, 2, 3)] + [((3, 1), 0)]
        self.DOWN = [((0, 0), q) for q in (1, 0, 3, 2)] + [((1, 0), 1), ((1, 0), 3)] + [((0, 1), q) for q in (1, 0, 2, 3)] + [((1, 1), 1)]
        if halves:
            self.UP.append(((3, 1), 4))
            self.DOWN.append(((1, 1), 5))
        self.PAIR = {0: ((0, 0), 0), 2: ((0, 0), 1), 4: ((0, 0), 2), 6: ((0, 0), 3)}
        for n, q in enumerate(across):
            self.PAIR[8 + n] = ((2, 0), q)
        self.out, self.own, self.place, self.device = out, own, place, device
        self.send, self.recv, self.sibling = send, recv, sibling
        self.ids_out, self.ids_own, self.ids_place, self.ids_send, self.ids_recv = ids_out, ids_own, ids_place, ids_send, ids_recv
        self.count, self.here, self.ids_here, self.ids_sent = 0, set(), set(), []
        self.lines_with_ids = {(line, slab) for line, slab in IDS_ALONG}
        self.lines = {"up": [], "down": [], "pair": []}

    def tile(self, slab, q):
        return self.out.at[self.place(*slab), pl.ds(*PIECES[q])]

    def start(self, line, slab, q, ring, pair):
        sent = self.lines[line]
        if len(sent) >= self.WINDOW:
            sent[-self.WINDOW].wait_send()
        if slab != (0, 0):
            self.arrived(slab, min(q, 2) if q > 3 else q)
        there = ((slab[0] - ring) % 4, (slab[1] - pair) % 2)
        source = self.own.at[pl.ds(*PIECES[q])] if slab == (0, 0) else self.tile(slab, q)
        copy = pltpu.make_async_remote_copy(
            src_ref=source,
            dst_ref=self.tile(slab, q),
            send_sem=self.send.at[self.count],
            recv_sem=self.recv.at[(there[0] + 4 * there[1]) * len(PIECES) + q],
            device_id=self.device(ring, pair),
            device_id_type=MESH,
        )
        copy.start()
        self.count += 1
        sent.append(copy)
        if (line, slab) in self.lines_with_ids:
            self.lines_with_ids.remove((line, slab))
            self.start_ids(slab, there, ring, pair)

    def start_ids(self, slab, there, ring, pair):
        if slab != (0, 0):
            self.ids_arrived(slab)
        copy = pltpu.make_async_remote_copy(
            src_ref=self.ids_own if slab == (0, 0) else self.ids_out.at[self.ids_place(*slab)],
            dst_ref=self.ids_out.at[self.ids_place(*slab)],
            send_sem=self.ids_send.at[len(self.ids_sent)],
            recv_sem=self.ids_recv.at[there[0] + 4 * there[1]],
            device_id=self.device(ring, pair),
            device_id_type=MESH,
        )
        copy.start()
        self.ids_sent.append(copy)

    def ids_arrived(self, slab):
        if slab not in self.ids_here:
            self.ids_here.add(slab)
            here = self.ids_out.at[self.ids_place(*slab)]
            pltpu.make_async_copy(here, here, self.ids_recv.at[slab[0] + 4 * slab[1]]).wait()

    def arrived(self, slab, q):
        if (slab, q) in self.here:
            return
        self.here.add((slab, q))
        here = self.tile(slab, q)
        pltpu.make_async_copy(here, here, self.recv.at[(slab[0] + 4 * slab[1]) * len(PIECES) + q]).wait()
        if self.sibling is not None:
            self.sibling(self, slab, q)

    def tick(self, t):
        if t in self.PAIR:
            self.start("pair", *self.PAIR[t], 0, 1)
        if t < len(self.UP):
            self.start("up", *self.UP[t], 1, 0)
            self.start("down", *self.DOWN[t], 3, 0)
        if t == 8:
            self.start_ids((3, 1), (2, 1), 1, 0)
        if 2 <= t < len(self.UP) + 2:
            (ring, pair), q = self.UP[t - 2]
            self.arrived(((ring + 3) % 4, pair), q)
            (ring, pair), q = self.DOWN[t - 2]
            self.arrived(((ring + 1) % 4, pair), q)
        if t - 3 in self.PAIR:
            slab, q = self.PAIR[t - 3]
            self.arrived((slab[0], 1), q)

    def finish(self):
        for line in self.lines.values():
            for copy in line[-self.WINDOW:]:
                copy.wait_send()
        for copy in self.ids_sent:
            copy.wait_send()


def gather_kernel(left, right, left_slots, right_slots, left_all, right_all, left_ids, right_ids,
                  ids, slots, left_send, left_recv, right_send, right_recv, sib_send, sib_recv,
                  idl_send, idl_recv, idr_send, idr_recv, ids_sib, own_sem):
    row, col = lax.axis_index("row"), lax.axis_index("col")
    y_hi, z = row // 4, lax.rem(row, 4)
    core, x, y_lo = lax.rem(col, 2), lax.rem(col // 2, 4), col // 8

    def left_place(ring, pair):
        return (lax.rem(y_lo + pair, 2) * 4 + lax.rem(x + ring, 4)) * 2 + core

    def right_place(ring, pair):
        return lax.rem(y_hi + pair, 2) * 4 + lax.rem(z + ring, 4)

    other = (row, col + 1 - 2 * core)

    fetch = [
        pltpu.make_async_copy(left_slots, slots.at[pl.ds(0, 1)], own_sem.at[4]),
        pltpu.make_async_copy(right_slots, slots.at[pl.ds(1, 1)], own_sem.at[5]),
    ]
    for copy in fetch:
        copy.start()
    barrier = pltpu.get_barrier_semaphore()
    for peer in (
        (row, left_place(1, 0)), (row, left_place(3, 0)), (row, left_place(0, 1)), other,
        (right_place(1, 0), col), (right_place(3, 0), col), (right_place(0, 1), col),
    ):
        pl.semaphore_signal(barrier, inc=1, device_id=peer, device_id_type=MESH)

    lane = lax.broadcasted_iota(jnp.int32, (1, LANES), 1)
    for copy in fetch:
        copy.wait()
    row_ids = jnp.full((1, LANES), -1, jnp.int32)
    for s in range(CAP):
        row_ids = jnp.where(lane == s, slots[0, s], row_ids)
        row_ids = jnp.where(lane == CAP + s, slots[1, s], row_ids)
    ids[...] = row_ids

    pl.semaphore_wait(barrier, 7)

    shared = []

    def to_sibling(factor, slab, q):
        index = (slab[0] + 4 * slab[1]) * 4 + q
        part = factor.tile(slab, q)
        copy = pltpu.make_async_remote_copy(
            src_ref=factor.own.at[pl.ds(q * TILE, TILE)] if slab == (0, 0) else part,
            dst_ref=part,
            send_sem=sib_send.at[index],
            recv_sem=sib_recv.at[index],
            device_id=other,
            device_id_type=MESH,
        )
        copy.start()
        shared.append(copy)

    def left_ids_place(ring, pair):
        return core * N_ROW + left_place(ring, pair) // 2

    lf = Factor(
        left_all, left, left_place, lambda ring, pair: (row, left_place(ring, pair)), left_send, left_recv, to_sibling,
        left_ids, ids, left_ids_place, idl_send, idl_recv, (2, 3),
    )
    rf = Factor(
        right_all, right, right_place, lambda ring, pair: (right_place(ring, pair), col), right_send, right_recv, None,
        right_ids, ids, right_place, idr_send, idr_recv, (3,),
    )

    lf.tick(0)
    rf.tick(0)
    lf.tick(1)
    rf.tick(1)

    for q in range(CAP):
        to_sibling(lf, (0, 0), q)
    local = [
        pltpu.make_async_copy(left, left_all.at[col], own_sem.at[0]),
        pltpu.make_async_copy(right, right_all.at[row], own_sem.at[1]),
        pltpu.make_async_copy(ids, left_ids.at[left_ids_place(0, 0)], own_sem.at[2]),
        pltpu.make_async_copy(ids, right_ids.at[row], own_sem.at[3]),
    ]
    for copy in local:
        copy.start()

    slabs = [(ring, pair) for pair in range(2) for ring in range(4)][1:]
    for t in range(2, 14):
        lf.tick(t)
        if t == 12:
            for copy in local:
                copy.wait()
            for slab in slabs:
                lf.ids_arrived(slab)
            block = left_ids.at[pl.ds(core * N_ROW, N_ROW)]
            copy = pltpu.make_async_remote_copy(
                src_ref=block, dst_ref=block, send_sem=ids_sib.at[0], recv_sem=ids_sib.at[1], device_id=other, device_id_type=MESH)
            copy.start()
            shared.append(copy)
        rf.tick(t)
    for slab in slabs:
        rf.ids_arrived(slab)

    for index in range(8 * CAP):
        ring, pair, q = index // 4 % 4, index // 16, index % 4
        place = left_place(ring, pair) + 1 - 2 * core
        part = left_all.at[place, pl.ds(q * TILE, TILE)]
        pltpu.make_async_copy(part, part, sib_recv.at[index]).wait()
    theirs = left_ids.at[pl.ds((1 - core) * N_ROW, N_ROW)]
    pltpu.make_async_copy(theirs, theirs, ids_sib.at[1]).wait()
    for copy in shared:
        copy.wait_send()
    lf.finish()
    rf.finish()


def gather(left, right, left_slots, right_slots):
    dma = pltpu.SemaphoreType.DMA
    operands = [pltpu.with_memory_space_constraint(x, pltpu.HBM) for x in (left, right, left_slots, right_slots)]
    return pl.pallas_call(
        gather_kernel,
        out_shape=[
            jax.ShapeDtypeStruct((N_COL, SLAB, TILE), jnp.bfloat16),
            jax.ShapeDtypeStruct((N_ROW, SLAB, TILE), jnp.bfloat16),
            jax.ShapeDtypeStruct((N_COL, 1, LANES), jnp.int32),
            jax.ShapeDtypeStruct((N_ROW, 1, LANES), jnp.int32),
        ],
        in_specs=[ANY, ANY, ANY, ANY],
        out_specs=[ANY, ANY, ANY, ANY],
        scratch_shapes=[
            pltpu.VMEM((1, LANES), jnp.int32),
            pltpu.SMEM((2, CAP), jnp.int32),
            dma((28,)), dma((48,)), dma((29,)), dma((48,)), dma((32,)), dma((32,)),
            dma((7,)), dma((8,)), dma((7,)), dma((8,)), dma((2,)), dma((6,)),
        ],
        compiler_params=pltpu.CompilerParams(collective_id=0, has_side_effects=True, vmem_limit_bytes=2**20),
        name="gather_slabs",
    )(*operands)


PER_STEP = 8
HALF = TILE // 2


def product_kernel(left_ids, right_ids, left_all, right_all, expanded):
    expanded[...] = jnp.zeros_like(expanded)

    def inner(n, _):
        work = []
        for w in range(PER_STEP):
            q, s = n * (PER_STEP // CAP) + w // CAP, w % CAP
            held = right_ids[q, 0, CAP + s]
            kept = held >= 0
            held = jnp.where(kept, held, 0)
            parity = held // CB_DEV
            rows = []
            for u in range(CAP):
                i = left_ids[parity * N_ROW + q, 0, u]
                rows.append(jnp.where(kept & (i >= 0), i, RB_DEV))
            work.append((q, s, 2 * q + parity, lax.rem(held, CB_DEV), rows))
        for q, s, k, j, rows in work:
            weights = right_all[q, s * TILE : (s + 1) * TILE]
            for u, i in enumerate(rows):
                for h in range(TILE // HALF):
                    expanded[i * CB_DEV + j, h * HALF : (h + 1) * HALF] += jnp.dot(
                        left_all[k, u * TILE + h * HALF : u * TILE + (h + 1) * HALF], weights, preferred_element_type=jnp.float32
                    )
        return 0

    lax.fori_loop(0, N_ROW * CAP // PER_STEP, inner, 0)


def product(left_ids, right_ids, left_all, right_all):
    return pl.pallas_call(
        product_kernel,
        out_shape=jax.ShapeDtypeStruct(((RB_DEV + 1) * CB_DEV, TILE, TILE), jnp.float32),
        in_specs=[SMEM, SMEM, VMEM, VMEM],
        out_specs=VMEM,
        compiler_params=pltpu.CompilerParams(vmem_limit_bytes=4 * 2**20),
        name="tile_products",
    )(left_ids, right_ids, left_all, right_all)


def total_kernel(expanded, total, part, held, send, recv):
    row, col = lax.axis_index("row"), lax.axis_index("col")
    peers = [(lax.rem(row + step, N_ROW), col) for step in range(1, N_ROW)]
    barrier = pltpu.get_barrier_semaphore()
    for peer in peers:
        pl.semaphore_signal(barrier, inc=1, device_id=peer, device_id_type=MESH)

    for j in range(CB_DEV):

        def add(i, sums):
            rows = expanded[i * CB_DEV + j]
            return sums + jnp.sum((rows * rows).reshape(TILE // 16, 16, TILE), axis=0)

        sums = lax.fori_loop(0, RB_DEV, add, jnp.zeros((16, TILE), jnp.float32))
        part[:, j * TILE : (j + 1) * TILE] = jnp.sum(sums, axis=0, keepdims=True)
    pl.semaphore_wait(barrier, N_ROW - 1)
    copies = []
    for n, peer in enumerate(peers):
        copy = pltpu.make_async_remote_copy(
            src_ref=part, dst_ref=held.at[n], send_sem=send.at[n], recv_sem=recv.at[n],
            device_id=peer, device_id_type=MESH)
        copy.start()
        copies.append(copy)
    value = part[...]
    for n, copy in enumerate(copies):
        copy.wait_recv()
        value = value + held[n]
    total[...] = value
    for copy in copies:
        copy.wait_send()


def column_total(expanded):
    dma = pltpu.SemaphoreType.DMA
    shape = (1, CB_DEV * TILE)
    return pl.pallas_call(
        total_kernel,
        out_shape=jax.ShapeDtypeStruct(shape, jnp.float32),
        in_specs=[VMEM],
        out_specs=VMEM,
        scratch_shapes=[
            pltpu.VMEM(shape, jnp.float32), pltpu.VMEM((N_ROW - 1, *shape), jnp.float32), dma((N_ROW - 1,)), dma((N_ROW - 1,)),
        ],
        compiler_params=pltpu.CompilerParams(collective_id=1, has_side_effects=True, vmem_limit_bytes=2**20),
        name="column_total",
    )(expanded)


SCALE_ROWS = 128
SCALE_SLOTS = 4


def scale_kernel(total, expanded, out, scaled, sems):
    factor = 1.0 / (total[...] / (RB_DEV * TILE * N_ROW) + EPSILON)
    copies = []
    for n in range(RB_DEV * TILE // SCALE_ROWS):
        slot = n % SCALE_SLOTS
        if n >= SCALE_SLOTS:
            copies[n - SCALE_SLOTS].wait()
        i, first = n * SCALE_ROWS // TILE, n * SCALE_ROWS % TILE
        for j in range(CB_DEV):
            columns = slice(j * TILE, (j + 1) * TILE)
            value = expanded[i * CB_DEV + j, first : first + SCALE_ROWS]
            scaled[slot, :, columns] = value * value * factor[:, columns]
        copy = pltpu.make_async_copy(scaled.at[slot], out.at[pl.ds(n * SCALE_ROWS, SCALE_ROWS)], sems.at[slot])
        copy.start()
        copies.append(copy)
    for copy in copies[-SCALE_SLOTS:]:
        copy.wait()


def scale(total, expanded):
    rows, cols = RB_DEV * TILE, CB_DEV * TILE
    return pl.pallas_call(
        scale_kernel,
        out_shape=jax.ShapeDtypeStruct((rows, cols), jnp.float32),
        in_specs=[VMEM, VMEM],
        out_specs=ANY,
        scratch_shapes=[pltpu.VMEM((SCALE_SLOTS, SCALE_ROWS, cols), jnp.float32), pltpu.SemaphoreType.DMA((SCALE_SLOTS,))],
        compiler_params=pltpu.CompilerParams(vmem_limit_bytes=4 * 2**20),
        name="scale_columns",
    )(total, expanded)


def body(left_tiles, left_slots, right_tiles, right_slots):
    left = left_tiles.reshape(SLAB, TILE)
    right = right_tiles.reshape(SLAB, TILE)
    left_all, right_all, left_ids, right_ids = gather(
        left, right, left_slots.reshape(1, CAP), right_slots.reshape(1, CAP)
    )
    expanded = product(left_ids, right_ids, left_all, right_all)
    return scale(column_total(expanded), expanded)


def solution(mesh):
    placed = (P("row", "col", None), P("row", "col"), P("row", "col", None), P("row", "col"))
    return jax.shard_map(
        body, mesh=mesh, in_specs=placed, out_specs=P("row", "col"), check_vma=False
    )
```

```python
import functools

import jax
import jax.numpy as jnp
from jax import lax
from jax.experimental import pallas as pl
from jax.experimental.pallas import tpu as pltpu
from jax.sharding import PartitionSpec as P

TILE = 256
RB_DEV = 8
CB_DEV = 4
CAP = 4
N_ROW = 8
N_COL = 16
SLAB = CAP * TILE
LANES = 128
EPSILON = 1e-06
EXPANDED = ((RB_DEV + 1) * CB_DEV, TILE, TILE)
MESH = pl.DeviceIdType.MESH
ANY = pl.BlockSpec(memory_space=pl.ANY)
VMEM = pl.BlockSpec(memory_space=pltpu.VMEM)
SMEM = pl.BlockSpec(memory_space=pltpu.SMEM)


IDS_ALONG = [("pair", (0, 0)), ("up", (0, 0)), ("up", (3, 0)), ("up", (0, 1)), ("down", (0, 0)), ("down", (0, 1))]
PIECES = [(0, TILE), (TILE, TILE), (2 * TILE, TILE), (3 * TILE, TILE), (2 * TILE, TILE // 2), (2 * TILE + TILE // 2, TILE // 2)]


class Factor:
    WINDOW = 2

    def __init__(self, out, own, place, device, send, recv, sibling, ids_out, ids_own, ids_place, ids_send, ids_recv, across):
        self.across = across
        halves = 2 not in across
        self.UP = [((0, 0), q) for q in (0, 1, 2, 3)] + [((3, 0), 0), ((3, 0), 2)] + [((0, 1), q) for q in (0, 1, 2, 3)] + [((3, 1), 0)]
        self.DOWN = [((0, 0), q) for q in (1, 0, 3, 2)] + [((1, 0), 1), ((1, 0), 3)] + [((0, 1), q) for q in (1, 0, 2, 3)] + [((1, 1), 1)]
        if halves:
            self.UP.append(((3, 1), 4))
            self.DOWN.append(((1, 1), 5))
        self.PAIR = {0: ((0, 0), 0), 2: ((0, 0), 1), 4: ((0, 0), 2), 6: ((0, 0), 3)}
        for n, q in enumerate(across):
            self.PAIR[8 + n] = ((2, 0), q)
        self.out, self.own, self.place, self.device = out, own, place, device
        self.send, self.recv, self.sibling = send, recv, sibling
        self.ids_out, self.ids_own, self.ids_place, self.ids_send, self.ids_recv = ids_out, ids_own, ids_place, ids_send, ids_recv
        self.count, self.here, self.ids_here, self.ids_sent = 0, set(), set(), []
        self.lines_with_ids = {(line, slab) for line, slab in IDS_ALONG}
        self.lines = {"up": [], "down": [], "pair": []}

    def tile(self, slab, q):
        return self.out.at[self.place(*slab), pl.ds(*PIECES[q])]

    def start(self, line, slab, q, ring, pair):
        sent = self.lines[line]
        if len(sent) >= self.WINDOW:
            sent[-self.WINDOW].wait_send()
        if slab != (0, 0):
            self.arrived(slab, min(q, 2) if q > 3 else q)
        there = ((slab[0] - ring) % 4, (slab[1] - pair) % 2)
        source = self.own.at[pl.ds(*PIECES[q])] if slab == (0, 0) else self.tile(slab, q)
        copy = pltpu.make_async_remote_copy(
            src_ref=source,
            dst_ref=self.tile(slab, q),
            send_sem=self.send.at[self.count],
            recv_sem=self.recv.at[(there[0] + 4 * there[1]) * len(PIECES) + q],
            device_id=self.device(ring, pair),
            device_id_type=MESH,
        )
        copy.start()
        self.count += 1
        sent.append(copy)
        if (line, slab) in self.lines_with_ids:
            self.lines_with_ids.remove((line, slab))
            self.start_ids(slab, there, ring, pair)

    def start_ids(self, slab, there, ring, pair):
        if slab != (0, 0):
            self.ids_arrived(slab)
        copy = pltpu.make_async_remote_copy(
            src_ref=self.ids_own if slab == (0, 0) else self.ids_out.at[self.ids_place(*slab)],
            dst_ref=self.ids_out.at[self.ids_place(*slab)],
            send_sem=self.ids_send.at[len(self.ids_sent)],
            recv_sem=self.ids_recv.at[there[0] + 4 * there[1]],
            device_id=self.device(ring, pair),
            device_id_type=MESH,
        )
        copy.start()
        self.ids_sent.append(copy)

    def ids_arrived(self, slab):
        if slab not in self.ids_here:
            self.ids_here.add(slab)
            here = self.ids_out.at[self.ids_place(*slab)]
            pltpu.make_async_copy(here, here, self.ids_recv.at[slab[0] + 4 * slab[1]]).wait()

    def arrived(self, slab, q):
        if (slab, q) in self.here:
            return
        self.here.add((slab, q))
        here = self.tile(slab, q)
        pltpu.make_async_copy(here, here, self.recv.at[(slab[0] + 4 * slab[1]) * len(PIECES) + q]).wait()
        if self.sibling is not None:
            self.sibling(self, slab, q)

    def tick(self, t):
        if t in self.PAIR:
            self.start("pair", *self.PAIR[t], 0, 1)
        if t < len(self.UP):
            self.start("up", *self.UP[t], 1, 0)
            self.start("down", *self.DOWN[t], 3, 0)
        if t == 8:
            self.start_ids((3, 1), (2, 1), 1, 0)
        if 2 <= t < len(self.UP) + 2:
            (ring, pair), q = self.UP[t - 2]
            self.arrived(((ring + 3) % 4, pair), q)
            (ring, pair), q = self.DOWN[t - 2]
            self.arrived(((ring + 1) % 4, pair), q)
        if t - 3 in self.PAIR:
            slab, q = self.PAIR[t - 3]
            self.arrived((slab[0], 1), q)

    def finish(self):
        for line in self.lines.values():
            for copy in line[-self.WINDOW:]:
                copy.wait_send()
        for copy in self.ids_sent:
            copy.wait_send()


def gather_kernel(left, right, left_slots, right_slots, left_all, right_all, left_ids, right_ids, blank,
                  ids, slots, left_send, left_recv, right_send, right_recv, sib_send, sib_recv,
                  idl_send, idl_recv, idr_send, idr_recv, ids_sib, own_sem):
    row, col = lax.axis_index("row"), lax.axis_index("col")
    y_hi, z = row // 4, lax.rem(row, 4)
    core, x, y_lo = lax.rem(col, 2), lax.rem(col // 2, 4), col // 8

    def left_place(ring, pair):
        return (lax.rem(y_lo + pair, 2) * 4 + lax.rem(x + ring, 4)) * 2 + core

    def right_place(ring, pair):
        return lax.rem(y_hi + pair, 2) * 4 + lax.rem(z + ring, 4)

    other = (row, col + 1 - 2 * core)

    fetch = [
        pltpu.make_async_copy(left_slots, slots.at[pl.ds(0, 1)], own_sem.at[4]),
        pltpu.make_async_copy(right_slots, slots.at[pl.ds(1, 1)], own_sem.at[5]),
    ]
    for copy in fetch:
        copy.start()
    barrier = pltpu.get_barrier_semaphore()
    for peer in (
        (row, left_place(1, 0)), (row, left_place(3, 0)), (row, left_place(0, 1)), other,
        (right_place(1, 0), col), (right_place(3, 0), col), (right_place(0, 1), col),
    ):
        pl.semaphore_signal(barrier, inc=1, device_id=peer, device_id_type=MESH)

    lane = lax.broadcasted_iota(jnp.int32, (1, LANES), 1)
    for copy in fetch:
        copy.wait()
    row_ids = jnp.full((1, LANES), -1, jnp.int32)
    for s in range(CAP):
        row_ids = jnp.where(lane == s, slots[0, s], row_ids)
        row_ids = jnp.where(lane == CAP + s, slots[1, s], row_ids)
    ids[...] = row_ids

    pl.semaphore_wait(barrier, 7)

    shared = []

    def to_sibling(factor, slab, q):
        index = (slab[0] + 4 * slab[1]) * 4 + q
        part = factor.tile(slab, q)
        copy = pltpu.make_async_remote_copy(
            src_ref=factor.own.at[pl.ds(q * TILE, TILE)] if slab == (0, 0) else part,
            dst_ref=part,
            send_sem=sib_send.at[index],
            recv_sem=sib_recv.at[index],
            device_id=other,
            device_id_type=MESH,
        )
        copy.start()
        shared.append(copy)

    def left_ids_place(ring, pair):
        return core * N_ROW + left_place(ring, pair) // 2

    lf = Factor(
        left_all, left, left_place, lambda ring, pair: (row, left_place(ring, pair)), left_send, left_recv, to_sibling,
        left_ids, ids, left_ids_place, idl_send, idl_recv, (2, 3),
    )
    rf = Factor(
        right_all, right, right_place, lambda ring, pair: (right_place(ring, pair), col), right_send, right_recv, None,
        right_ids, ids, right_place, idr_send, idr_recv, (3,),
    )

    lf.tick(0)
    rf.tick(0)
    lf.tick(1)
    rf.tick(1)

    for q in range(CAP):
        to_sibling(lf, (0, 0), q)
    local = [
        pltpu.make_async_copy(left, left_all.at[col], own_sem.at[0]),
        pltpu.make_async_copy(right, right_all.at[row], own_sem.at[1]),
        pltpu.make_async_copy(ids, left_ids.at[left_ids_place(0, 0)], own_sem.at[2]),
        pltpu.make_async_copy(ids, right_ids.at[row], own_sem.at[3]),
    ]
    for copy in local:
        copy.start()

    @pl.loop(0, EXPANDED[0])
    def _(n):
        blank[n] = jnp.zeros(EXPANDED[1:], jnp.float32)

    slabs = [(ring, pair) for pair in range(2) for ring in range(4)][1:]
    for t in range(2, 14):
        lf.tick(t)
        if t == 12:
            for copy in local:
                copy.wait()
            for slab in slabs:
                lf.ids_arrived(slab)
            block = left_ids.at[pl.ds(core * N_ROW, N_ROW)]
            copy = pltpu.make_async_remote_copy(
                src_ref=block, dst_ref=block, send_sem=ids_sib.at[0], recv_sem=ids_sib.at[1], device_id=other, device_id_type=MESH)
            copy.start()
            shared.append(copy)
        rf.tick(t)
    for slab in slabs:
        rf.ids_arrived(slab)

    for index in range(8 * CAP):
        ring, pair, q = index // 4 % 4, index // 16, index % 4
        place = left_place(ring, pair) + 1 - 2 * core
        part = left_all.at[place, pl.ds(q * TILE, TILE)]
        pltpu.make_async_copy(part, part, sib_recv.at[index]).wait()
    theirs = left_ids.at[pl.ds((1 - core) * N_ROW, N_ROW)]
    pltpu.make_async_copy(theirs, theirs, ids_sib.at[1]).wait()
    for copy in shared:
        copy.wait_send()
    lf.finish()
    rf.finish()


def gather(left, right, left_slots, right_slots):
    dma = pltpu.SemaphoreType.DMA
    operands = [pltpu.with_memory_space_constraint(x, pltpu.HBM) for x in (left, right, left_slots, right_slots)]
    return pl.pallas_call(
        gather_kernel,
        out_shape=[
            jax.ShapeDtypeStruct((N_COL, SLAB, TILE), jnp.bfloat16),
            jax.ShapeDtypeStruct((N_ROW, SLAB, TILE), jnp.bfloat16),
            jax.ShapeDtypeStruct((N_COL, 1, LANES), jnp.int32),
            jax.ShapeDtypeStruct((N_ROW, 1, LANES), jnp.int32),
            pltpu.VMEM(EXPANDED, jnp.float32),
        ],
        in_specs=[ANY, ANY, ANY, ANY],
        out_specs=[ANY, ANY, ANY, ANY, VMEM],
        scratch_shapes=[
            pltpu.VMEM((1, LANES), jnp.int32),
            pltpu.SMEM((2, CAP), jnp.int32),
            dma((28,)), dma((48,)), dma((29,)), dma((48,)), dma((32,)), dma((32,)),
            dma((7,)), dma((8,)), dma((7,)), dma((8,)), dma((2,)), dma((6,)),
        ],
        compiler_params=pltpu.CompilerParams(collective_id=0, has_side_effects=True, vmem_limit_bytes=2**20),
        name="gather_slabs",
    )(*operands)


PER_STEP = 8
HALF = TILE // 2


def product_kernel(left_ids, right_ids, left_all, right_all, blank, expanded):
    def inner(n, _):
        work = []
        for w in range(PER_STEP):
            q, s = n * (PER_STEP // CAP) + w // CAP, w % CAP
            held = right_ids[q, 0, CAP + s]
            kept = held >= 0
            held = jnp.where(kept, held, 0)
            parity = held // CB_DEV
            rows = []
            for u in range(CAP):
                i = left_ids[parity * N_ROW + q, 0, u]
                rows.append(jnp.where(kept & (i >= 0), i, RB_DEV))
            work.append((q, s, 2 * q + parity, lax.rem(held, CB_DEV), rows))
        for q, s, k, j, rows in work:
            weights = right_all[q, s * TILE : (s + 1) * TILE]
            for u, i in enumerate(rows):
                for h in range(TILE // HALF):
                    expanded[i * CB_DEV + j, h * HALF : (h + 1) * HALF] += jnp.dot(
                        left_all[k, u * TILE + h * HALF : u * TILE + (h + 1) * HALF], weights, preferred_element_type=jnp.float32
                    )
        return 0

    lax.fori_loop(0, N_ROW * CAP // PER_STEP, inner, 0)


def product(left_ids, right_ids, left_all, right_all, blank):
    return pl.pallas_call(
        product_kernel,
        out_shape=pltpu.VMEM(EXPANDED, jnp.float32),
        in_specs=[SMEM, SMEM, VMEM, VMEM, VMEM],
        out_specs=VMEM,
        input_output_aliases={4: 0},
        compiler_params=pltpu.CompilerParams(vmem_limit_bytes=4 * 2**20),
        name="tile_products",
    )(left_ids, right_ids, left_all, right_all, blank)


def total_kernel(expanded, total, part, held, send, recv):
    row, col = lax.axis_index("row"), lax.axis_index("col")
    peers = [(lax.rem(row + step, N_ROW), col) for step in range(1, N_ROW)]
    barrier = pltpu.get_barrier_semaphore()
    for peer in peers:
        pl.semaphore_signal(barrier, inc=1, device_id=peer, device_id_type=MESH)

    for j in range(CB_DEV):

        def add(i, sums):
            rows = expanded[i * CB_DEV + j]
            return sums + jnp.sum((rows * rows).reshape(TILE // 16, 16, TILE), axis=0)

        sums = lax.fori_loop(0, RB_DEV, add, jnp.zeros((16, TILE), jnp.float32))
        part[:, j * TILE : (j + 1) * TILE] = jnp.sum(sums, axis=0, keepdims=True)
    pl.semaphore_wait(barrier, N_ROW - 1)
    copies = []
    for n, peer in enumerate(peers):
        copy = pltpu.make_async_remote_copy(
            src_ref=part, dst_ref=held.at[n], send_sem=send.at[n], recv_sem=recv.at[n],
            device_id=peer, device_id_type=MESH)
        copy.start()
        copies.append(copy)
    value = part[...]
    for n, copy in enumerate(copies):
        copy.wait_recv()
        value = value + held[n]
    total[...] = value
    for copy in copies:
        copy.wait_send()


def column_total(expanded):
    dma = pltpu.SemaphoreType.DMA
    shape = (1, CB_DEV * TILE)
    return pl.pallas_call(
        total_kernel,
        out_shape=jax.ShapeDtypeStruct(shape, jnp.float32),
        in_specs=[VMEM],
        out_specs=VMEM,
        scratch_shapes=[
            pltpu.VMEM(shape, jnp.float32), pltpu.VMEM((N_ROW - 1, *shape), jnp.float32), dma((N_ROW - 1,)), dma((N_ROW - 1,)),
        ],
        compiler_params=pltpu.CompilerParams(collective_id=1, has_side_effects=True, vmem_limit_bytes=2**20),
        name="column_total",
    )(expanded)


SCALE_ROWS = 256
SCALE_SLOTS = 4


def scale_kernel(total, expanded, out, scaled, sems):
    factor = 1.0 / (total[...] / (RB_DEV * TILE * N_ROW) + EPSILON)
    copies = []
    for n in range(RB_DEV * TILE // SCALE_ROWS):
        slot = n % SCALE_SLOTS
        if n >= SCALE_SLOTS:
            copies[n - SCALE_SLOTS].wait()
        i, first = n * SCALE_ROWS // TILE, n * SCALE_ROWS % TILE
        for j in range(CB_DEV):
            columns = slice(j * TILE, (j + 1) * TILE)
            value = expanded[i * CB_DEV + j, first : first + SCALE_ROWS]
            scaled[slot, :, columns] = value * value * factor[:, columns]
        copy = pltpu.make_async_copy(scaled.at[slot], out.at[pl.ds(n * SCALE_ROWS, SCALE_ROWS)], sems.at[slot])
        copy.start()
        copies.append(copy)
    for copy in copies[-SCALE_SLOTS:]:
        copy.wait()


def scale(total, expanded):
    rows, cols = RB_DEV * TILE, CB_DEV * TILE
    return pl.pallas_call(
        scale_kernel,
        out_shape=jax.ShapeDtypeStruct((rows, cols), jnp.float32),
        in_specs=[VMEM, VMEM],
        out_specs=ANY,
        scratch_shapes=[pltpu.VMEM((SCALE_SLOTS, SCALE_ROWS, cols), jnp.float32), pltpu.SemaphoreType.DMA((SCALE_SLOTS,))],
        compiler_params=pltpu.CompilerParams(vmem_limit_bytes=6 * 2**20),
        name="scale_columns",
    )(total, expanded)


def body(left_tiles, left_slots, right_tiles, right_slots):
    left = left_tiles.reshape(SLAB, TILE)
    right = right_tiles.reshape(SLAB, TILE)
    left_all, right_all, left_ids, right_ids, blank = gather(
        left, right, left_slots.reshape(1, CAP), right_slots.reshape(1, CAP)
    )
    expanded = product(left_ids, right_ids, left_all, right_all, blank)
    return scale(column_total(expanded), expanded)


def solution(mesh):
    placed = (P("row", "col", None), P("row", "col"), P("row", "col", None), P("row", "col"))
    return jax.shard_map(
        body, mesh=mesh, in_specs=placed, out_specs=P("row", "col"), check_vma=False
    )
```

```python
import functools

import jax
import jax.numpy as jnp
from jax import lax
from jax.experimental import pallas as pl
from jax.experimental.pallas import tpu as pltpu
from jax.sharding import PartitionSpec as P

TILE = 256
RB_DEV = 8
CB_DEV = 4
CAP = 4
N_ROW = 8
N_COL = 16
SLAB = CAP * TILE
LANES = 128
EPSILON = 1e-06
EXPANDED = ((RB_DEV + 1) * CB_DEV, TILE, TILE)
MESH = pl.DeviceIdType.MESH
ANY = pl.BlockSpec(memory_space=pl.ANY)
VMEM = pl.BlockSpec(memory_space=pltpu.VMEM)
SMEM = pl.BlockSpec(memory_space=pltpu.SMEM)


IDS_TICKS = {
    1: [((0, 0), 1, 0), ((0, 0), 3, 0), ((0, 0), 0, 1)],
    3: [((3, 0), 1, 0)],
    4: [((0, 1), 1, 0), ((0, 1), 3, 0)],
    6: [((3, 1), 1, 0)],
}
PIECES = [(0, TILE), (TILE, TILE), (2 * TILE, TILE), (3 * TILE, TILE), (2 * TILE, TILE // 2), (2 * TILE + TILE // 2, TILE // 2)]


class Factor:
    WINDOW = 2

    def __init__(self, out, own, place, device, send, recv, sibling, ids_out, ids_own, ids_place, ids_send, ids_recv, across):
        self.across = across
        halves = 2 not in across
        self.UP = [((0, 0), q) for q in (0, 1, 2, 3)] + [((3, 0), 0), ((3, 0), 2)] + [((0, 1), q) for q in (0, 1, 2, 3)] + [((3, 1), 0)]
        self.DOWN = [((0, 0), q) for q in (1, 0, 3, 2)] + [((1, 0), 1), ((1, 0), 3)] + [((0, 1), q) for q in (1, 0, 2, 3)] + [((1, 1), 1)]
        if halves:
            self.UP.append(((3, 1), 4))
            self.DOWN.append(((1, 1), 5))
        self.PAIR = {0: ((0, 0), 0), 2: ((0, 0), 1), 4: ((0, 0), 2), 6: ((0, 0), 3)}
        for n, q in enumerate(across):
            self.PAIR[8 + n] = ((2, 0), q)
        self.out, self.own, self.place, self.device = out, own, place, device
        self.send, self.recv, self.sibling = send, recv, sibling
        self.ids_out, self.ids_own, self.ids_place, self.ids_send, self.ids_recv = ids_out, ids_own, ids_place, ids_send, ids_recv
        self.count, self.here, self.ids_here, self.ids_sent = 0, set(), set(), []
        self.lines = {"up": [], "down": [], "pair": []}

    def tile(self, slab, q):
        return self.out.at[self.place(*slab), pl.ds(*PIECES[q])]

    def start(self, line, slab, q, ring, pair):
        sent = self.lines[line]
        if len(sent) >= self.WINDOW:
            sent[-self.WINDOW].wait_send()
        if slab != (0, 0):
            self.arrived(slab, min(q, 2) if q > 3 else q)
        there = ((slab[0] - ring) % 4, (slab[1] - pair) % 2)
        source = self.own.at[pl.ds(*PIECES[q])] if slab == (0, 0) else self.tile(slab, q)
        copy = pltpu.make_async_remote_copy(
            src_ref=source,
            dst_ref=self.tile(slab, q),
            send_sem=self.send.at[self.count],
            recv_sem=self.recv.at[(there[0] + 4 * there[1]) * len(PIECES) + q],
            device_id=self.device(ring, pair),
            device_id_type=MESH,
        )
        copy.start()
        self.count += 1
        sent.append(copy)

    def start_ids(self, slab, ring, pair):
        there = ((slab[0] - ring) % 4, (slab[1] - pair) % 2)
        if slab != (0, 0):
            self.ids_arrived(slab)
        copy = pltpu.make_async_remote_copy(
            src_ref=self.ids_own if slab == (0, 0) else self.ids_out.at[self.ids_place(*slab)],
            dst_ref=self.ids_out.at[self.ids_place(*slab)],
            send_sem=self.ids_send.at[len(self.ids_sent)],
            recv_sem=self.ids_recv.at[there[0] + 4 * there[1]],
            device_id=self.device(ring, pair),
            device_id_type=MESH,
        )
        copy.start()
        self.ids_sent.append(copy)

    def ids_arrived(self, slab):
        if slab not in self.ids_here:
            self.ids_here.add(slab)
            here = self.ids_out.at[self.ids_place(*slab)]
            pltpu.make_async_copy(here, here, self.ids_recv.at[slab[0] + 4 * slab[1]]).wait()

    def arrived(self, slab, q):
        if (slab, q) in self.here:
            return
        self.here.add((slab, q))
        here = self.tile(slab, q)
        pltpu.make_async_copy(here, here, self.recv.at[(slab[0] + 4 * slab[1]) * len(PIECES) + q]).wait()
        if self.sibling is not None:
            self.sibling(self, slab, q)

    def tick(self, t):
        if t in self.PAIR:
            self.start("pair", *self.PAIR[t], 0, 1)
        if t < len(self.UP):
            self.start("up", *self.UP[t], 1, 0)
            self.start("down", *self.DOWN[t], 3, 0)
        for way in IDS_TICKS.get(t, ()):
            self.start_ids(*way)
        if 2 <= t < len(self.UP) + 2:
            (ring, pair), q = self.UP[t - 2]
            self.arrived(((ring + 3) % 4, pair), q)
            (ring, pair), q = self.DOWN[t - 2]
            self.arrived(((ring + 1) % 4, pair), q)
        if t - 3 in self.PAIR:
            slab, q = self.PAIR[t - 3]
            self.arrived((slab[0], 1), q)

    def finish(self):
        for line in self.lines.values():
            for copy in line[-self.WINDOW:]:
                copy.wait_send()
        for copy in self.ids_sent:
            copy.wait_send()


def gather_kernel(left, right, left_slots, right_slots, left_all, right_all, left_ids, right_ids, blank,
                  ids, slots, left_send, left_recv, right_send, right_recv, sib_send, sib_recv,
                  idl_send, idl_recv, idr_send, idr_recv, ids_sib, own_sem):
    row, col = lax.axis_index("row"), lax.axis_index("col")
    y_hi, z = row // 4, lax.rem(row, 4)
    core, x, y_lo = lax.rem(col, 2), lax.rem(col // 2, 4), col // 8

    def left_place(ring, pair):
        return (lax.rem(y_lo + pair, 2) * 4 + lax.rem(x + ring, 4)) * 2 + core

    def right_place(ring, pair):
        return lax.rem(y_hi + pair, 2) * 4 + lax.rem(z + ring, 4)

    other = (row, col + 1 - 2 * core)

    fetch = [
        pltpu.make_async_copy(left_slots, slots.at[pl.ds(0, 1)], own_sem.at[4]),
        pltpu.make_async_copy(right_slots, slots.at[pl.ds(1, 1)], own_sem.at[5]),
    ]
    for copy in fetch:
        copy.start()
    barrier = pltpu.get_barrier_semaphore()
    for peer in (
        (row, left_place(1, 0)), (row, left_place(3, 0)), (row, left_place(0, 1)), other,
        (right_place(1, 0), col), (right_place(3, 0), col), (right_place(0, 1), col),
    ):
        pl.semaphore_signal(barrier, inc=1, device_id=peer, device_id_type=MESH)

    pl.semaphore_wait(barrier, 7)

    shared = []

    def to_sibling(factor, slab, q):
        index = (slab[0] + 4 * slab[1]) * 4 + q
        part = factor.tile(slab, q)
        copy = pltpu.make_async_remote_copy(
            src_ref=factor.own.at[pl.ds(q * TILE, TILE)] if slab == (0, 0) else part,
            dst_ref=part,
            send_sem=sib_send.at[index],
            recv_sem=sib_recv.at[index],
            device_id=other,
            device_id_type=MESH,
        )
        copy.start()
        shared.append(copy)

    def left_ids_place(ring, pair):
        return core * N_ROW + left_place(ring, pair) // 2

    lf = Factor(
        left_all, left, left_place, lambda ring, pair: (row, left_place(ring, pair)), left_send, left_recv, to_sibling,
        left_ids, ids, left_ids_place, idl_send, idl_recv, (2, 3),
    )
    rf = Factor(
        right_all, right, right_place, lambda ring, pair: (right_place(ring, pair), col), right_send, right_recv, None,
        right_ids, ids, right_place, idr_send, idr_recv, (3,),
    )

    lf.tick(0)
    rf.tick(0)

    lane = lax.broadcasted_iota(jnp.int32, (1, LANES), 1)
    for copy in fetch:
        copy.wait()
    row_ids = jnp.full((1, LANES), -1, jnp.int32)
    for s in range(CAP):
        row_ids = jnp.where(lane == s, slots[0, s], row_ids)
        row_ids = jnp.where(lane == CAP + s, slots[1, s], row_ids)
    ids[...] = row_ids

    lf.tick(1)
    rf.tick(1)

    for q in range(CAP):
        to_sibling(lf, (0, 0), q)
    local = [
        pltpu.make_async_copy(left, left_all.at[col], own_sem.at[0]),
        pltpu.make_async_copy(right, right_all.at[row], own_sem.at[1]),
        pltpu.make_async_copy(ids, left_ids.at[left_ids_place(0, 0)], own_sem.at[2]),
        pltpu.make_async_copy(ids, right_ids.at[row], own_sem.at[3]),
    ]
    for copy in local:
        copy.start()

    @pl.loop(0, EXPANDED[0])
    def _(n):
        blank[n] = jnp.zeros(EXPANDED[1:], jnp.float32)

    slabs = [(ring, pair) for pair in range(2) for ring in range(4)][1:]
    for t in range(2, 14):
        lf.tick(t)
        if t == 12:
            for copy in local:
                copy.wait()
            for slab in slabs:
                lf.ids_arrived(slab)
            block = left_ids.at[pl.ds(core * N_ROW, N_ROW)]
            copy = pltpu.make_async_remote_copy(
                src_ref=block, dst_ref=block, send_sem=ids_sib.at[0], recv_sem=ids_sib.at[1], device_id=other, device_id_type=MESH)
            copy.start()
            shared.append(copy)
        rf.tick(t)
    for slab in slabs:
        rf.ids_arrived(slab)

    for index in range(8 * CAP):
        ring, pair, q = index // 4 % 4, index // 16, index % 4
        place = left_place(ring, pair) + 1 - 2 * core
        part = left_all.at[place, pl.ds(q * TILE, TILE)]
        pltpu.make_async_copy(part, part, sib_recv.at[index]).wait()
    theirs = left_ids.at[pl.ds((1 - core) * N_ROW, N_ROW)]
    pltpu.make_async_copy(theirs, theirs, ids_sib.at[1]).wait()
    for copy in shared:
        copy.wait_send()
    lf.finish()
    rf.finish()


def gather(left, right, left_slots, right_slots):
    dma = pltpu.SemaphoreType.DMA
    operands = [pltpu.with_memory_space_constraint(x, pltpu.HBM) for x in (left, right, left_slots, right_slots)]
    return pl.pallas_call(
        gather_kernel,
        out_shape=[
            jax.ShapeDtypeStruct((N_COL, SLAB, TILE), jnp.bfloat16),
            jax.ShapeDtypeStruct((N_ROW, SLAB, TILE), jnp.bfloat16),
            jax.ShapeDtypeStruct((N_COL, 1, LANES), jnp.int32),
            jax.ShapeDtypeStruct((N_ROW, 1, LANES), jnp.int32),
            pltpu.VMEM(EXPANDED, jnp.float32),
        ],
        in_specs=[ANY, ANY, ANY, ANY],
        out_specs=[ANY, ANY, ANY, ANY, VMEM],
        scratch_shapes=[
            pltpu.VMEM((1, LANES), jnp.int32),
            pltpu.SMEM((2, CAP), jnp.int32),
            dma((28,)), dma((48,)), dma((29,)), dma((48,)), dma((32,)), dma((32,)),
            dma((7,)), dma((8,)), dma((7,)), dma((8,)), dma((2,)), dma((6,)),
        ],
        compiler_params=pltpu.CompilerParams(collective_id=0, has_side_effects=True, vmem_limit_bytes=2**20),
        name="gather_slabs",
    )(*operands)


PER_STEP = 16
HALF = TILE // 2


def product_kernel(left_ids, right_ids, left_all, right_all, blank, expanded):
    def inner(n, _):
        work = []
        for w in range(PER_STEP):
            q, s = n * (PER_STEP // CAP) + w // CAP, w % CAP
            held = right_ids[q, 0, CAP + s]
            kept = held >= 0
            held = jnp.where(kept, held, 0)
            parity = held // CB_DEV
            rows = []
            for u in range(CAP):
                i = left_ids[parity * N_ROW + q, 0, u]
                rows.append(jnp.where(kept & (i >= 0), i, RB_DEV))
            work.append((q, s, 2 * q + parity, lax.rem(held, CB_DEV), rows))
        for q, s, k, j, rows in work:
            weights = right_all[q, s * TILE : (s + 1) * TILE]
            for u, i in enumerate(rows):
                for h in range(TILE // HALF):
                    expanded[i * CB_DEV + j, h * HALF : (h + 1) * HALF] += jnp.dot(
                        left_all[k, u * TILE + h * HALF : u * TILE + (h + 1) * HALF], weights, preferred_element_type=jnp.float32
                    )
        return 0

    lax.fori_loop(0, N_ROW * CAP // PER_STEP, inner, 0)


def product(left_ids, right_ids, left_all, right_all, blank):
    return pl.pallas_call(
        product_kernel,
        out_shape=pltpu.VMEM(EXPANDED, jnp.float32),
        in_specs=[SMEM, SMEM, VMEM, VMEM, VMEM],
        out_specs=VMEM,
        input_output_aliases={4: 0},
        compiler_params=pltpu.CompilerParams(vmem_limit_bytes=4 * 2**20),
        name="tile_products",
    )(left_ids, right_ids, left_all, right_all, blank)


def total_kernel(expanded, total, part, held, send, recv):
    row, col = lax.axis_index("row"), lax.axis_index("col")
    peers = [(lax.rem(row + step, N_ROW), col) for step in range(1, N_ROW)]
    barrier = pltpu.get_barrier_semaphore()
    for peer in peers:
        pl.semaphore_signal(barrier, inc=1, device_id=peer, device_id_type=MESH)

    for j in range(CB_DEV):

        def add(i, sums):
            rows = expanded[i * CB_DEV + j]
            return sums + jnp.sum((rows * rows).reshape(TILE // 16, 16, TILE), axis=0)

        sums = lax.fori_loop(0, RB_DEV, add, jnp.zeros((16, TILE), jnp.float32))
        part[:, j * TILE : (j + 1) * TILE] = jnp.sum(sums, axis=0, keepdims=True)
    pl.semaphore_wait(barrier, N_ROW - 1)
    copies = []
    for n, peer in enumerate(peers):
        copy = pltpu.make_async_remote_copy(
            src_ref=part, dst_ref=held.at[n], send_sem=send.at[n], recv_sem=recv.at[n],
            device_id=peer, device_id_type=MESH)
        copy.start()
        copies.append(copy)
    value = part[...]
    for n, copy in enumerate(copies):
        copy.wait_recv()
        value = value + held[n]
    total[...] = value
    for copy in copies:
        copy.wait_send()


def column_total(expanded):
    dma = pltpu.SemaphoreType.DMA
    shape = (1, CB_DEV * TILE)
    return pl.pallas_call(
        total_kernel,
        out_shape=jax.ShapeDtypeStruct(shape, jnp.float32),
        in_specs=[VMEM],
        out_specs=VMEM,
        scratch_shapes=[
            pltpu.VMEM(shape, jnp.float32), pltpu.VMEM((N_ROW - 1, *shape), jnp.float32), dma((N_ROW - 1,)), dma((N_ROW - 1,)),
        ],
        compiler_params=pltpu.CompilerParams(collective_id=1, has_side_effects=True, vmem_limit_bytes=2**20),
        name="column_total",
    )(expanded)


SCALE_BLOCKS = [TILE // 4, TILE // 4, TILE // 2] + [TILE] * (RB_DEV - 1)
SCALE_SLOTS = 4


def scale_kernel(total, expanded, out, scaled, sems):
    factor = 1.0 / (total[...] / (RB_DEV * TILE * N_ROW) + EPSILON)
    copies, done = [], 0
    for n, count in enumerate(SCALE_BLOCKS):
        slot = n % SCALE_SLOTS
        if n >= SCALE_SLOTS:
            copies[n - SCALE_SLOTS].wait()
        i, first = done // TILE, done % TILE
        for j in range(CB_DEV):
            columns = slice(j * TILE, (j + 1) * TILE)
            value = expanded[i * CB_DEV + j, first : first + count]
            scaled[slot, :count, columns] = value * value * factor[:, columns]
        copy = pltpu.make_async_copy(scaled.at[slot, pl.ds(0, count)], out.at[pl.ds(done, count)], sems.at[slot])
        copy.start()
        copies.append(copy)
        done += count
    for copy in copies[-SCALE_SLOTS:]:
        copy.wait()


def scale(total, expanded):
    rows, cols = RB_DEV * TILE, CB_DEV * TILE
    return pl.pallas_call(
        scale_kernel,
        out_shape=jax.ShapeDtypeStruct((rows, cols), jnp.float32),
        in_specs=[VMEM, VMEM],
        out_specs=ANY,
        scratch_shapes=[pltpu.VMEM((SCALE_SLOTS, TILE, cols), jnp.float32), pltpu.SemaphoreType.DMA((SCALE_SLOTS,))],
        compiler_params=pltpu.CompilerParams(vmem_limit_bytes=6 * 2**20),
        name="scale_columns",
    )(total, expanded)


def body(left_tiles, left_slots, right_tiles, right_slots):
    left = left_tiles.reshape(SLAB, TILE)
    right = right_tiles.reshape(SLAB, TILE)
    left_all, right_all, left_ids, right_ids, blank = gather(
        left, right, left_slots.reshape(1, CAP), right_slots.reshape(1, CAP)
    )
    expanded = product(left_ids, right_ids, left_all, right_all, blank)
    return scale(column_total(expanded), expanded)


def solution(mesh):
    placed = (P("row", "col", None), P("row", "col"), P("row", "col", None), P("row", "col"))
    return jax.shard_map(
        body, mesh=mesh, in_specs=placed, out_specs=P("row", "col"), check_vma=False
    )
```

```python
import functools

import jax
import jax.numpy as jnp
from jax import lax
from jax.experimental import pallas as pl
from jax.experimental.pallas import tpu as pltpu
from jax.sharding import PartitionSpec as P

TILE = 256
RB_DEV = 8
CB_DEV = 4
CAP = 4
N_ROW = 8
N_COL = 16
SLAB = CAP * TILE
LANES = 128
EPSILON = 1e-06
EXPANDED = ((RB_DEV + 1) * CB_DEV, TILE, TILE)
MESH = pl.DeviceIdType.MESH
ANY = pl.BlockSpec(memory_space=pl.ANY)
VMEM = pl.BlockSpec(memory_space=pltpu.VMEM)
SMEM = pl.BlockSpec(memory_space=pltpu.SMEM)


IDS_TICKS = {
    1: [((0, 0), 1, 0), ((0, 0), 3, 0), ((0, 0), 0, 1)],
    3: [((3, 0), 1, 0)],
    4: [((0, 1), 1, 0), ((0, 1), 3, 0)],
    6: [((3, 1), 1, 0)],
}
PIECES = [(0, TILE), (TILE, TILE), (2 * TILE, TILE), (3 * TILE, TILE), (2 * TILE, TILE // 2), (2 * TILE + TILE // 2, TILE // 2)]


class Factor:
    WINDOW = 2

    def __init__(self, out, own, place, device, send, recv, sibling, ids_out, ids_own, ids_place, ids_send, ids_recv, across):
        self.across = across
        halves = 2 not in across
        self.UP = [((0, 0), q) for q in (0, 1, 2, 3)] + [((3, 0), 0), ((3, 0), 2)] + [((0, 1), q) for q in (0, 1, 2, 3)] + [((3, 1), 0)]
        self.DOWN = [((0, 0), q) for q in (1, 0, 3, 2)] + [((1, 0), 1), ((1, 0), 3)] + [((0, 1), q) for q in (1, 0, 2, 3)] + [((1, 1), 1)]
        if halves:
            self.UP.append(((3, 1), 4))
            self.DOWN.append(((1, 1), 5))
        self.PAIR = {0: ((0, 0), 0), 2: ((0, 0), 1), 4: ((0, 0), 2), 6: ((0, 0), 3)}
        for n, q in enumerate(across):
            self.PAIR[8 + n] = ((2, 0), q)
        self.out, self.own, self.place, self.device = out, own, place, device
        self.send, self.recv, self.sibling = send, recv, sibling
        self.ids_out, self.ids_own, self.ids_place, self.ids_send, self.ids_recv = ids_out, ids_own, ids_place, ids_send, ids_recv
        self.count, self.here, self.ids_here, self.ids_sent = 0, set(), set(), []
        self.lines = {"up": [], "down": [], "pair": []}

    def tile(self, slab, q):
        return self.out.at[self.place(*slab), pl.ds(*PIECES[q])]

    def start(self, line, slab, q, ring, pair):
        sent = self.lines[line]
        if len(sent) >= self.WINDOW:
            sent[-self.WINDOW].wait_send()
        if slab != (0, 0):
            self.arrived(slab, min(q, 2) if q > 3 else q)
        there = ((slab[0] - ring) % 4, (slab[1] - pair) % 2)
        source = self.own.at[pl.ds(*PIECES[q])] if slab == (0, 0) else self.tile(slab, q)
        copy = pltpu.make_async_remote_copy(
            src_ref=source,
            dst_ref=self.tile(slab, q),
            send_sem=self.send.at[self.count],
            recv_sem=self.recv.at[(there[0] + 4 * there[1]) * len(PIECES) + q],
            device_id=self.device(ring, pair),
            device_id_type=MESH,
        )
        copy.start()
        self.count += 1
        sent.append(copy)

    def start_ids(self, slab, ring, pair):
        there = ((slab[0] - ring) % 4, (slab[1] - pair) % 2)
        if slab != (0, 0):
            self.ids_arrived(slab)
        copy = pltpu.make_async_remote_copy(
            src_ref=self.ids_own if slab == (0, 0) else self.ids_out.at[self.ids_place(*slab)],
            dst_ref=self.ids_out.at[self.ids_place(*slab)],
            send_sem=self.ids_send.at[len(self.ids_sent)],
            recv_sem=self.ids_recv.at[there[0] + 4 * there[1]],
            device_id=self.device(ring, pair),
            device_id_type=MESH,
        )
        copy.start()
        self.ids_sent.append(copy)

    def ids_arrived(self, slab):
        if slab not in self.ids_here:
            self.ids_here.add(slab)
            here = self.ids_out.at[self.ids_place(*slab)]
            pltpu.make_async_copy(here, here, self.ids_recv.at[slab[0] + 4 * slab[1]]).wait()

    def arrived(self, slab, q):
        if (slab, q) in self.here:
            return
        self.here.add((slab, q))
        here = self.tile(slab, q)
        pltpu.make_async_copy(here, here, self.recv.at[(slab[0] + 4 * slab[1]) * len(PIECES) + q]).wait()
        if self.sibling is not None:
            self.sibling(self, slab, q)

    def tick(self, t):
        if t in self.PAIR:
            self.start("pair", *self.PAIR[t], 0, 1)
        if t < len(self.UP):
            self.start("up", *self.UP[t], 1, 0)
            self.start("down", *self.DOWN[t], 3, 0)
        for way in IDS_TICKS.get(t, ()):
            self.start_ids(*way)
        if 2 <= t < len(self.UP) + 2:
            (ring, pair), q = self.UP[t - 2]
            self.arrived(((ring + 3) % 4, pair), q)
            (ring, pair), q = self.DOWN[t - 2]
            self.arrived(((ring + 1) % 4, pair), q)
        if t - 3 in self.PAIR:
            slab, q = self.PAIR[t - 3]
            self.arrived((slab[0], 1), q)

    def finish(self):
        for line in self.lines.values():
            for copy in line[-self.WINDOW:]:
                copy.wait_send()
        for copy in self.ids_sent:
            copy.wait_send()


def gather_kernel(left, right, left_slots, right_slots, left_all, right_all, all_ids, blank,
                  ids, slots, left_send, left_recv, right_send, right_recv, sib_send, sib_recv,
                  idl_send, idl_recv, idr_send, idr_recv, ids_sib, own_sem):
    row, col = lax.axis_index("row"), lax.axis_index("col")
    y_hi, z = row // 4, lax.rem(row, 4)
    core, x, y_lo = lax.rem(col, 2), lax.rem(col // 2, 4), col // 8

    def left_place(ring, pair):
        return (lax.rem(y_lo + pair, 2) * 4 + lax.rem(x + ring, 4)) * 2 + core

    def right_place(ring, pair):
        return lax.rem(y_hi + pair, 2) * 4 + lax.rem(z + ring, 4)

    other = (row, col + 1 - 2 * core)

    fetch = [
        pltpu.make_async_copy(left_slots, slots.at[pl.ds(0, 1)], own_sem.at[4]),
        pltpu.make_async_copy(right_slots, slots.at[pl.ds(1, 1)], own_sem.at[5]),
    ]
    for copy in fetch:
        copy.start()
    barrier = pltpu.get_barrier_semaphore()
    for peer in (
        (row, left_place(1, 0)), (row, left_place(3, 0)), (row, left_place(0, 1)), other,
        (right_place(1, 0), col), (right_place(3, 0), col), (right_place(0, 1), col),
    ):
        pl.semaphore_signal(barrier, inc=1, device_id=peer, device_id_type=MESH)

    pl.semaphore_wait(barrier, 7)

    shared = []

    def to_sibling(factor, slab, q):
        index = (slab[0] + 4 * slab[1]) * 4 + q
        part = factor.tile(slab, q)
        copy = pltpu.make_async_remote_copy(
            src_ref=factor.own.at[pl.ds(q * TILE, TILE)] if slab == (0, 0) else part,
            dst_ref=part,
            send_sem=sib_send.at[index],
            recv_sem=sib_recv.at[index],
            device_id=other,
            device_id_type=MESH,
        )
        copy.start()
        shared.append(copy)

    def left_ids_place(ring, pair):
        return core * N_ROW + left_place(ring, pair) // 2

    lf = Factor(
        left_all, left, left_place, lambda ring, pair: (row, left_place(ring, pair)), left_send, left_recv, to_sibling,
        all_ids, ids, left_ids_place, idl_send, idl_recv, (2, 3),
    )
    rf = Factor(
        right_all, right, right_place, lambda ring, pair: (right_place(ring, pair), col), right_send, right_recv, None,
        all_ids, ids, lambda ring, pair: N_COL + right_place(ring, pair), idr_send, idr_recv, (3,),
    )

    lf.tick(0)
    rf.tick(0)

    lane = lax.broadcasted_iota(jnp.int32, (1, LANES), 1)
    for copy in fetch:
        copy.wait()
    row_ids = jnp.full((1, LANES), -1, jnp.int32)
    for s in range(CAP):
        row_ids = jnp.where(lane == s, slots[0, s], row_ids)
        row_ids = jnp.where(lane == CAP + s, slots[1, s], row_ids)
    ids[...] = row_ids

    lf.tick(1)
    rf.tick(1)

    for q in range(CAP):
        to_sibling(lf, (0, 0), q)
    local = [
        pltpu.make_async_copy(left, left_all.at[col], own_sem.at[0]),
        pltpu.make_async_copy(right, right_all.at[row], own_sem.at[1]),
        pltpu.make_async_copy(ids, all_ids.at[left_ids_place(0, 0)], own_sem.at[2]),
        pltpu.make_async_copy(ids, all_ids.at[N_COL + row], own_sem.at[3]),
    ]
    for copy in local:
        copy.start()

    @pl.loop(0, EXPANDED[0])
    def _(n):
        blank[n] = jnp.zeros(EXPANDED[1:], jnp.float32)

    slabs = [(ring, pair) for pair in range(2) for ring in range(4)][1:]
    for t in range(2, 14):
        lf.tick(t)
        if t == 10:
            for copy in local:
                copy.wait()
            for slab in slabs:
                lf.ids_arrived(slab)
            block = all_ids.at[pl.ds(core * N_ROW, N_ROW)]
            copy = pltpu.make_async_remote_copy(
                src_ref=block, dst_ref=block, send_sem=ids_sib.at[0], recv_sem=ids_sib.at[1], device_id=other, device_id_type=MESH)
            copy.start()
            shared.append(copy)
        rf.tick(t)
    for slab in slabs:
        rf.ids_arrived(slab)

    for index in range(8 * CAP):
        ring, pair, q = index // 4 % 4, index // 16, index % 4
        place = left_place(ring, pair) + 1 - 2 * core
        part = left_all.at[place, pl.ds(q * TILE, TILE)]
        pltpu.make_async_copy(part, part, sib_recv.at[index]).wait()
    theirs = all_ids.at[pl.ds((1 - core) * N_ROW, N_ROW)]
    pltpu.make_async_copy(theirs, theirs, ids_sib.at[1]).wait()
    for copy in shared:
        copy.wait_send()
    lf.finish()
    rf.finish()


def gather(left, right, left_slots, right_slots):
    dma = pltpu.SemaphoreType.DMA
    operands = [pltpu.with_memory_space_constraint(x, pltpu.HBM) for x in (left, right, left_slots, right_slots)]
    return pl.pallas_call(
        gather_kernel,
        out_shape=[
            jax.ShapeDtypeStruct((N_COL, SLAB, TILE), jnp.bfloat16),
            jax.ShapeDtypeStruct((N_ROW, SLAB, TILE), jnp.bfloat16),
            jax.ShapeDtypeStruct((N_COL + N_ROW, 1, LANES), jnp.int32),
            pltpu.VMEM(EXPANDED, jnp.float32),
        ],
        in_specs=[ANY, ANY, ANY, ANY],
        out_specs=[ANY, ANY, ANY, VMEM],
        scratch_shapes=[
            pltpu.VMEM((1, LANES), jnp.int32),
            pltpu.SMEM((2, CAP), jnp.int32),
            dma((28,)), dma((48,)), dma((29,)), dma((48,)), dma((32,)), dma((32,)),
            dma((7,)), dma((8,)), dma((7,)), dma((8,)), dma((2,)), dma((6,)),
        ],
        compiler_params=pltpu.CompilerParams(collective_id=0, has_side_effects=True, vmem_limit_bytes=2**20),
        name="gather_slabs",
    )(*operands)


PER_STEP = 16
HALF = TILE // 2


def product_kernel(all_ids, left_all, right_all, blank, expanded):
    def inner(n, _):
        work = []
        for w in range(PER_STEP):
            q, s = n * (PER_STEP // CAP) + w // CAP, w % CAP
            held = all_ids[N_COL + q, 0, CAP + s]
            kept = held >= 0
            held = jnp.where(kept, held, 0)
            parity = held // CB_DEV
            rows = []
            for u in range(CAP):
                i = all_ids[parity * N_ROW + q, 0, u]
                rows.append(jnp.where(kept & (i >= 0), i, RB_DEV))
            work.append((q, s, 2 * q + parity, lax.rem(held, CB_DEV), rows))
        for q, s, k, j, rows in work:
            weights = right_all[q, s * TILE : (s + 1) * TILE]
            for u, i in enumerate(rows):
                for h in range(TILE // HALF):
                    expanded[i * CB_DEV + j, h * HALF : (h + 1) * HALF] += jnp.dot(
                        left_all[k, u * TILE + h * HALF : u * TILE + (h + 1) * HALF], weights, preferred_element_type=jnp.float32
                    )
        return 0

    lax.fori_loop(0, N_ROW * CAP // PER_STEP, inner, 0)


def product(all_ids, left_all, right_all, blank):
    return pl.pallas_call(
        product_kernel,
        out_shape=pltpu.VMEM(EXPANDED, jnp.float32),
        in_specs=[SMEM, VMEM, VMEM, VMEM],
        out_specs=VMEM,
        input_output_aliases={3: 0},
        compiler_params=pltpu.CompilerParams(vmem_limit_bytes=4 * 2**20),
        name="tile_products",
    )(all_ids, left_all, right_all, blank)


def total_kernel(expanded, total, part, held, send, recv):
    row, col = lax.axis_index("row"), lax.axis_index("col")
    peers = [(lax.rem(row + step, N_ROW), col) for step in range(1, N_ROW)]
    barrier = pltpu.get_barrier_semaphore()
    for peer in peers:
        pl.semaphore_signal(barrier, inc=1, device_id=peer, device_id_type=MESH)

    for j in range(CB_DEV):

        def add(i, sums):
            rows = expanded[i * CB_DEV + j]
            return sums + jnp.sum((rows * rows).reshape(TILE // 16, 16, TILE), axis=0)

        sums = lax.fori_loop(0, RB_DEV, add, jnp.zeros((16, TILE), jnp.float32))
        part[:, j * TILE : (j + 1) * TILE] = jnp.sum(sums, axis=0, keepdims=True)
    pl.semaphore_wait(barrier, N_ROW - 1)
    copies = []
    for n, peer in enumerate(peers):
        copy = pltpu.make_async_remote_copy(
            src_ref=part, dst_ref=held.at[n], send_sem=send.at[n], recv_sem=recv.at[n],
            device_id=peer, device_id_type=MESH)
        copy.start()
        copies.append(copy)
    value = part[...]
    for n, copy in enumerate(copies):
        copy.wait_recv()
        value = value + held[n]
    total[...] = value
    for copy in copies:
        copy.wait_send()


def column_total(expanded):
    dma = pltpu.SemaphoreType.DMA
    shape = (1, CB_DEV * TILE)
    return pl.pallas_call(
        total_kernel,
        out_shape=jax.ShapeDtypeStruct(shape, jnp.float32),
        in_specs=[VMEM],
        out_specs=VMEM,
        scratch_shapes=[
            pltpu.VMEM(shape, jnp.float32), pltpu.VMEM((N_ROW - 1, *shape), jnp.float32), dma((N_ROW - 1,)), dma((N_ROW - 1,)),
        ],
        compiler_params=pltpu.CompilerParams(collective_id=1, has_side_effects=True, vmem_limit_bytes=2**20),
        name="column_total",
    )(expanded)


SCALE_BLOCKS = [TILE] * RB_DEV
SCALE_SLOTS = 4


def scale_kernel(total, expanded, out, scaled, sems):
    factor = 1.0 / (total[...] / (RB_DEV * TILE * N_ROW) + EPSILON)
    copies, done = [], 0
    for n, count in enumerate(SCALE_BLOCKS):
        slot = n % SCALE_SLOTS
        if n >= SCALE_SLOTS:
            copies[n - SCALE_SLOTS].wait()
        i, first = done // TILE, done % TILE
        for j in range(CB_DEV):
            columns = slice(j * TILE, (j + 1) * TILE)
            value = expanded[i * CB_DEV + j, first : first + count]
            scaled[slot, :count, columns] = value * value * factor[:, columns]
        copy = pltpu.make_async_copy(scaled.at[slot, pl.ds(0, count)], out.at[pl.ds(done, count)], sems.at[slot])
        copy.start()
        copies.append(copy)
        done += count
    for copy in copies[-SCALE_SLOTS:]:
        copy.wait()


def scale(total, expanded):
    rows, cols = RB_DEV * TILE, CB_DEV * TILE
    return pl.pallas_call(
        scale_kernel,
        out_shape=jax.ShapeDtypeStruct((rows, cols), jnp.float32),
        in_specs=[VMEM, VMEM],
        out_specs=ANY,
        scratch_shapes=[pltpu.VMEM((SCALE_SLOTS, TILE, cols), jnp.float32), pltpu.SemaphoreType.DMA((SCALE_SLOTS,))],
        compiler_params=pltpu.CompilerParams(vmem_limit_bytes=6 * 2**20),
        name="scale_columns",
    )(total, expanded)


def body(left_tiles, left_slots, right_tiles, right_slots):
    left = left_tiles.reshape(SLAB, TILE)
    right = right_tiles.reshape(SLAB, TILE)
    left_all, right_all, all_ids, blank = gather(
        left, right, left_slots.reshape(1, CAP), right_slots.reshape(1, CAP)
    )
    expanded = product(all_ids, left_all, right_all, blank)
    return scale(column_total(expanded), expanded)


def solution(mesh):
    placed = (P("row", "col", None), P("row", "col"), P("row", "col", None), P("row", "col"))
    return jax.shard_map(
        body, mesh=mesh, in_specs=placed, out_specs=P("row", "col"), check_vma=False
    )
```

```python
import functools

import jax
import jax.numpy as jnp
from jax import lax
from jax.experimental import pallas as pl
from jax.experimental.pallas import tpu as pltpu
from jax.sharding import PartitionSpec as P

TILE = 256
RB_DEV = 8
CB_DEV = 4
CAP = 4
N_ROW = 8
N_COL = 16
SLAB = CAP * TILE
LANES = 128
EPSILON = 1e-06
EXPANDED = ((RB_DEV + 1) * CB_DEV, TILE, TILE)
MESH = pl.DeviceIdType.MESH
ANY = pl.BlockSpec(memory_space=pl.ANY)
VMEM = pl.BlockSpec(memory_space=pltpu.VMEM)
SMEM = pl.BlockSpec(memory_space=pltpu.SMEM)


IDS_TICKS = {
    1: [((0, 0), 1, 0), ((0, 0), 3, 0), ((0, 0), 0, 1)],
    3: [((3, 0), 1, 0)],
    4: [((0, 1), 1, 0), ((0, 1), 3, 0)],
    6: [((3, 1), 1, 0)],
}
PIECES = [(0, TILE), (TILE, TILE), (2 * TILE, TILE), (3 * TILE, TILE), (2 * TILE, TILE // 2), (2 * TILE + TILE // 2, TILE // 2)]


class Factor:
    WINDOW = 3

    def __init__(self, out, own, place, device, send, recv, sibling, ids_out, ids_own, ids_place, ids_send, ids_recv, across):
        self.across = across
        halves = 2 not in across
        self.UP = [((0, 0), q) for q in (0, 1, 2, 3)] + [((3, 0), 0), ((3, 0), 2)] + [((0, 1), q) for q in (0, 1, 2, 3)] + [((3, 1), 0)]
        self.DOWN = [((0, 0), q) for q in (1, 0, 3, 2)] + [((1, 0), 1), ((1, 0), 3)] + [((0, 1), q) for q in (1, 0, 2, 3)] + [((1, 1), 1)]
        if halves:
            self.UP.append(((3, 1), 4))
            self.DOWN.append(((1, 1), 5))
        self.PAIR = {0: ((0, 0), 0), 2: ((0, 0), 1), 4: ((0, 0), 2), 6: ((0, 0), 3)}
        for n, q in enumerate(across):
            self.PAIR[8 + n] = ((2, 0), q)
        self.out, self.own, self.place, self.device = out, own, place, device
        self.send, self.recv, self.sibling = send, recv, sibling
        self.ids_out, self.ids_own, self.ids_place, self.ids_send, self.ids_recv = ids_out, ids_own, ids_place, ids_send, ids_recv
        self.count, self.here, self.ids_here, self.ids_sent = 0, set(), set(), []
        self.lines = {"up": [], "down": [], "pair": []}

    def tile(self, slab, q):
        return self.out.at[self.place(*slab), pl.ds(*PIECES[q])]

    def start(self, line, slab, q, ring, pair):
        sent = self.lines[line]
        if len(sent) >= self.WINDOW:
            sent[-self.WINDOW].wait_send()
        if slab != (0, 0):
            self.arrived(slab, min(q, 2) if q > 3 else q)
        there = ((slab[0] - ring) % 4, (slab[1] - pair) % 2)
        source = self.own.at[pl.ds(*PIECES[q])] if slab == (0, 0) else self.tile(slab, q)
        copy = pltpu.make_async_remote_copy(
            src_ref=source,
            dst_ref=self.tile(slab, q),
            send_sem=self.send.at[self.count],
            recv_sem=self.recv.at[(there[0] + 4 * there[1]) * len(PIECES) + q],
            device_id=self.device(ring, pair),
            device_id_type=MESH,
        )
        copy.start()
        self.count += 1
        sent.append(copy)

    def start_ids(self, slab, ring, pair):
        there = ((slab[0] - ring) % 4, (slab[1] - pair) % 2)
        if slab != (0, 0):
            self.ids_arrived(slab)
        copy = pltpu.make_async_remote_copy(
            src_ref=self.ids_own if slab == (0, 0) else self.ids_out.at[self.ids_place(*slab)],
            dst_ref=self.ids_out.at[self.ids_place(*slab)],
            send_sem=self.ids_send.at[len(self.ids_sent)],
            recv_sem=self.ids_recv.at[there[0] + 4 * there[1]],
            device_id=self.device(ring, pair),
            device_id_type=MESH,
        )
        copy.start()
        self.ids_sent.append(copy)

    def ids_arrived(self, slab):
        if slab not in self.ids_here:
            self.ids_here.add(slab)
            here = self.ids_out.at[self.ids_place(*slab)]
            pltpu.make_async_copy(here, here, self.ids_recv.at[slab[0] + 4 * slab[1]]).wait()

    def arrived(self, slab, q):
        if (slab, q) in self.here:
            return
        self.here.add((slab, q))
        here = self.tile(slab, q)
        pltpu.make_async_copy(here, here, self.recv.at[(slab[0] + 4 * slab[1]) * len(PIECES) + q]).wait()
        if self.sibling is not None:
            self.sibling(self, slab, q)

    def tick(self, t):
        if t in self.PAIR:
            self.start("pair", *self.PAIR[t], 0, 1)
        if t < len(self.UP):
            self.start("up", *self.UP[t], 1, 0)
            self.start("down", *self.DOWN[t], 3, 0)
        for way in IDS_TICKS.get(t, ()):
            self.start_ids(*way)
        if 2 <= t < len(self.UP) + 2:
            (ring, pair), q = self.UP[t - 2]
            self.arrived(((ring + 3) % 4, pair), q)
            (ring, pair), q = self.DOWN[t - 2]
            self.arrived(((ring + 1) % 4, pair), q)
        if t - 3 in self.PAIR:
            slab, q = self.PAIR[t - 3]
            self.arrived((slab[0], 1), q)

    def finish(self):
        for line in self.lines.values():
            for copy in line[-self.WINDOW:]:
                copy.wait_send()
        for copy in self.ids_sent:
            copy.wait_send()


def gather_kernel(left, right, left_slots, right_slots, left_all, right_all, all_ids, blank,
                  ids, slots, left_send, left_recv, right_send, right_recv, sib_send, sib_recv,
                  idl_send, idl_recv, idr_send, idr_recv, ids_sib, own_sem):
    row, col = lax.axis_index("row"), lax.axis_index("col")
    y_hi, z = row // 4, lax.rem(row, 4)
    core, x, y_lo = lax.rem(col, 2), lax.rem(col // 2, 4), col // 8

    def left_place(ring, pair):
        return (lax.rem(y_lo + pair, 2) * 4 + lax.rem(x + ring, 4)) * 2 + core

    def right_place(ring, pair):
        return lax.rem(y_hi + pair, 2) * 4 + lax.rem(z + ring, 4)

    other = (row, col + 1 - 2 * core)

    fetch = [
        pltpu.make_async_copy(left_slots, slots.at[pl.ds(0, 1)], own_sem.at[4]),
        pltpu.make_async_copy(right_slots, slots.at[pl.ds(1, 1)], own_sem.at[5]),
    ]
    for copy in fetch:
        copy.start()
    barrier = pltpu.get_barrier_semaphore()
    for peer in (
        (row, left_place(1, 0)), (row, left_place(3, 0)), (row, left_place(0, 1)), other,
        (right_place(1, 0), col), (right_place(3, 0), col), (right_place(0, 1), col),
    ):
        pl.semaphore_signal(barrier, inc=1, device_id=peer, device_id_type=MESH)

    pl.semaphore_wait(barrier, 7)

    shared = []

    def to_sibling(factor, slab, q):
        index = (slab[0] + 4 * slab[1]) * 4 + q
        part = factor.tile(slab, q)
        copy = pltpu.make_async_remote_copy(
            src_ref=factor.own.at[pl.ds(q * TILE, TILE)] if slab == (0, 0) else part,
            dst_ref=part,
            send_sem=sib_send.at[index],
            recv_sem=sib_recv.at[index],
            device_id=other,
            device_id_type=MESH,
        )
        copy.start()
        shared.append(copy)

    def left_ids_place(ring, pair):
        return core * N_ROW + left_place(ring, pair) // 2

    lf = Factor(
        left_all, left, left_place, lambda ring, pair: (row, left_place(ring, pair)), left_send, left_recv, to_sibling,
        all_ids, ids, left_ids_place, idl_send, idl_recv, (2, 3),
    )
    rf = Factor(
        right_all, right, right_place, lambda ring, pair: (right_place(ring, pair), col), right_send, right_recv, None,
        all_ids, ids, lambda ring, pair: N_COL + right_place(ring, pair), idr_send, idr_recv, (3,),
    )

    lf.tick(0)
    rf.tick(0)

    lane = lax.broadcasted_iota(jnp.int32, (1, LANES), 1)
    for copy in fetch:
        copy.wait()
    row_ids = jnp.full((1, LANES), -1, jnp.int32)
    for s in range(CAP):
        row_ids = jnp.where(lane == s, slots[0, s], row_ids)
        row_ids = jnp.where(lane == CAP + s, slots[1, s], row_ids)
    ids[...] = row_ids

    lf.tick(1)
    rf.tick(1)

    for q in range(CAP):
        to_sibling(lf, (0, 0), q)
    local = [
        pltpu.make_async_copy(left, left_all.at[col], own_sem.at[0]),
        pltpu.make_async_copy(right, right_all.at[row], own_sem.at[1]),
        pltpu.make_async_copy(ids, all_ids.at[left_ids_place(0, 0)], own_sem.at[2]),
        pltpu.make_async_copy(ids, all_ids.at[N_COL + row], own_sem.at[3]),
    ]
    for copy in local:
        copy.start()

    @pl.loop(0, EXPANDED[0])
    def _(n):
        blank[n] = jnp.zeros(EXPANDED[1:], jnp.float32)

    slabs = [(ring, pair) for pair in range(2) for ring in range(4)][1:]
    for t in range(2, 14):
        lf.tick(t)
        if t == 10:
            for copy in local:
                copy.wait()
            for slab in slabs:
                lf.ids_arrived(slab)
            block = all_ids.at[pl.ds(core * N_ROW, N_ROW)]
            copy = pltpu.make_async_remote_copy(
                src_ref=block, dst_ref=block, send_sem=ids_sib.at[0], recv_sem=ids_sib.at[1], device_id=other, device_id_type=MESH)
            copy.start()
            shared.append(copy)
        rf.tick(t)
    for slab in slabs:
        rf.ids_arrived(slab)

    for index in range(8 * CAP):
        ring, pair, q = index // 4 % 4, index // 16, index % 4
        place = left_place(ring, pair) + 1 - 2 * core
        part = left_all.at[place, pl.ds(q * TILE, TILE)]
        pltpu.make_async_copy(part, part, sib_recv.at[index]).wait()
    theirs = all_ids.at[pl.ds((1 - core) * N_ROW, N_ROW)]
    pltpu.make_async_copy(theirs, theirs, ids_sib.at[1]).wait()
    for copy in shared:
        copy.wait_send()
    lf.finish()
    rf.finish()


def gather(left, right, left_slots, right_slots):
    dma = pltpu.SemaphoreType.DMA
    operands = [pltpu.with_memory_space_constraint(x, pltpu.HBM) for x in (left, right, left_slots, right_slots)]
    return pl.pallas_call(
        gather_kernel,
        out_shape=[
            jax.ShapeDtypeStruct((N_COL, SLAB, TILE), jnp.bfloat16),
            jax.ShapeDtypeStruct((N_ROW, SLAB, TILE), jnp.bfloat16),
            jax.ShapeDtypeStruct((N_COL + N_ROW, 1, LANES), jnp.int32),
            pltpu.VMEM(EXPANDED, jnp.float32),
        ],
        in_specs=[ANY, ANY, ANY, ANY],
        out_specs=[ANY, ANY, ANY, VMEM],
        scratch_shapes=[
            pltpu.VMEM((1, LANES), jnp.int32),
            pltpu.SMEM((2, CAP), jnp.int32),
            dma((28,)), dma((48,)), dma((29,)), dma((48,)), dma((32,)), dma((32,)),
            dma((7,)), dma((8,)), dma((7,)), dma((8,)), dma((2,)), dma((6,)),
        ],
        compiler_params=pltpu.CompilerParams(collective_id=0, has_side_effects=True, vmem_limit_bytes=2**20),
        name="gather_slabs",
    )(*operands)


PER_STEP = 16
HALF = TILE // 2


def product_kernel(all_ids, left_all, right_all, blank, expanded):
    def inner(n, _):
        work = []
        for w in range(PER_STEP):
            q, s = n * (PER_STEP // CAP) + w // CAP, w % CAP
            held = all_ids[N_COL + q, 0, CAP + s]
            kept = held >= 0
            held = jnp.where(kept, held, 0)
            parity = held // CB_DEV
            rows = []
            for u in range(CAP):
                i = all_ids[parity * N_ROW + q, 0, u]
                rows.append(jnp.where(kept & (i >= 0), i, RB_DEV))
            work.append((q, s, 2 * q + parity, lax.rem(held, CB_DEV), rows))
        for q, s, k, j, rows in work:
            weights = right_all[q, s * TILE : (s + 1) * TILE]
            for u, i in enumerate(rows):
                for h in range(TILE // HALF):
                    expanded[i * CB_DEV + j, h * HALF : (h + 1) * HALF] += jnp.dot(
                        left_all[k, u * TILE + h * HALF : u * TILE + (h + 1) * HALF], weights, preferred_element_type=jnp.float32
                    )
        return 0

    lax.fori_loop(0, N_ROW * CAP // PER_STEP, inner, 0)


def product(all_ids, left_all, right_all, blank):
    return pl.pallas_call(
        product_kernel,
        out_shape=pltpu.VMEM(EXPANDED, jnp.float32),
        in_specs=[SMEM, VMEM, VMEM, VMEM],
        out_specs=VMEM,
        input_output_aliases={3: 0},
        compiler_params=pltpu.CompilerParams(vmem_limit_bytes=4 * 2**20),
        name="tile_products",
    )(all_ids, left_all, right_all, blank)


def total_kernel(expanded, total, part, held, send, recv):
    row, col = lax.axis_index("row"), lax.axis_index("col")
    peers = [(lax.rem(row + step, N_ROW), col) for step in range(1, N_ROW)]
    barrier = pltpu.get_barrier_semaphore()
    for peer in peers:
        pl.semaphore_signal(barrier, inc=1, device_id=peer, device_id_type=MESH)

    for j in range(CB_DEV):

        def add(i, sums):
            rows = expanded[i * CB_DEV + j]
            return sums + jnp.sum((rows * rows).reshape(TILE // 16, 16, TILE), axis=0)

        sums = lax.fori_loop(0, RB_DEV, add, jnp.zeros((16, TILE), jnp.float32))
        part[:, j * TILE : (j + 1) * TILE] = jnp.sum(sums, axis=0, keepdims=True)
    pl.semaphore_wait(barrier, N_ROW - 1)
    copies = []
    for n, peer in enumerate(peers):
        copy = pltpu.make_async_remote_copy(
            src_ref=part, dst_ref=held.at[n], send_sem=send.at[n], recv_sem=recv.at[n],
            device_id=peer, device_id_type=MESH)
        copy.start()
        copies.append(copy)
    value = part[...]
    for n, copy in enumerate(copies):
        copy.wait_recv()
        value = value + held[n]
    total[...] = value
    for copy in copies:
        copy.wait_send()


def column_total(expanded):
    dma = pltpu.SemaphoreType.DMA
    shape = (1, CB_DEV * TILE)
    return pl.pallas_call(
        total_kernel,
        out_shape=jax.ShapeDtypeStruct(shape, jnp.float32),
        in_specs=[VMEM],
        out_specs=VMEM,
        scratch_shapes=[
            pltpu.VMEM(shape, jnp.float32), pltpu.VMEM((N_ROW - 1, *shape), jnp.float32), dma((N_ROW - 1,)), dma((N_ROW - 1,)),
        ],
        compiler_params=pltpu.CompilerParams(collective_id=1, has_side_effects=True, vmem_limit_bytes=2**20),
        name="column_total",
    )(expanded)


SCALE_BLOCKS = [TILE] * RB_DEV
SCALE_SLOTS = 4


def scale_kernel(total, expanded, out, scaled, sems):
    factor = 1.0 / (total[...] / (RB_DEV * TILE * N_ROW) + EPSILON)
    copies, done = [], 0
    for n, count in enumerate(SCALE_BLOCKS):
        slot = n % SCALE_SLOTS
        if n >= SCALE_SLOTS:
            copies[n - SCALE_SLOTS].wait()
        i, first = done // TILE, done % TILE
        for j in range(CB_DEV):
            columns = slice(j * TILE, (j + 1) * TILE)
            value = expanded[i * CB_DEV + j, first : first + count]
            scaled[slot, :count, columns] = value * value * factor[:, columns]
        copy = pltpu.make_async_copy(scaled.at[slot, pl.ds(0, count)], out.at[pl.ds(done, count)], sems.at[slot])
        copy.start()
        copies.append(copy)
        done += count
    for copy in copies[-SCALE_SLOTS:]:
        copy.wait()


def scale(total, expanded):
    rows, cols = RB_DEV * TILE, CB_DEV * TILE
    return pl.pallas_call(
        scale_kernel,
        out_shape=jax.ShapeDtypeStruct((rows, cols), jnp.float32),
        in_specs=[VMEM, VMEM],
        out_specs=ANY,
        scratch_shapes=[pltpu.VMEM((SCALE_SLOTS, TILE, cols), jnp.float32), pltpu.SemaphoreType.DMA((SCALE_SLOTS,))],
        compiler_params=pltpu.CompilerParams(vmem_limit_bytes=6 * 2**20),
        name="scale_columns",
    )(total, expanded)


def body(left_tiles, left_slots, right_tiles, right_slots):
    left = left_tiles.reshape(SLAB, TILE)
    right = right_tiles.reshape(SLAB, TILE)
    left_all, right_all, all_ids, blank = gather(
        left, right, left_slots.reshape(1, CAP), right_slots.reshape(1, CAP)
    )
    expanded = product(all_ids, left_all, right_all, blank)
    return scale(column_total(expanded), expanded)


def solution(mesh):
    placed = (P("row", "col", None), P("row", "col"), P("row", "col", None), P("row", "col"))
    return jax.shard_map(
        body, mesh=mesh, in_specs=placed, out_specs=P("row", "col"), check_vma=False
    )
```

```python
import functools

import jax
import jax.numpy as jnp
from jax import lax
from jax.experimental import pallas as pl
from jax.experimental.pallas import tpu as pltpu
from jax.sharding import PartitionSpec as P

TILE = 256
RB_DEV = 8
CB_DEV = 4
CAP = 4
N_ROW = 8
N_COL = 16
SLAB = CAP * TILE
LANES = 128
EPSILON = 1e-06
EXPANDED = ((RB_DEV + 1) * CB_DEV, TILE, TILE)
MESH = pl.DeviceIdType.MESH
ANY = pl.BlockSpec(memory_space=pl.ANY)
VMEM = pl.BlockSpec(memory_space=pltpu.VMEM)
SMEM = pl.BlockSpec(memory_space=pltpu.SMEM)


IDS_TICKS = {
    1: [((0, 0), 1, 0), ((0, 0), 3, 0), ((0, 0), 0, 1)],
    3: [((3, 0), 1, 0)],
    4: [((0, 1), 1, 0), ((0, 1), 3, 0)],
    6: [((3, 1), 1, 0)],
}
PIECES = [(0, TILE), (TILE, TILE), (2 * TILE, TILE), (3 * TILE, TILE), (2 * TILE, TILE // 2), (2 * TILE + TILE // 2, TILE // 2)]


class Factor:
    WINDOW = 2

    def __init__(self, out, own, place, device, send, recv, sibling, ids_out, ids_own, ids_place, ids_send, ids_recv, across):
        self.across = across
        halves = 2 not in across
        self.UP = [((0, 0), q) for q in (0, 1, 2, 3)] + [((3, 0), 0), ((3, 0), 2)] + [((0, 1), q) for q in (0, 1, 2, 3)] + [((3, 1), 0)]
        self.DOWN = [((0, 0), q) for q in (1, 0, 3, 2)] + [((1, 0), 1), ((1, 0), 3)] + [((0, 1), q) for q in (1, 0, 2, 3)] + [((1, 1), 1)]
        if halves:
            self.UP.append(((3, 1), 4))
            self.DOWN.append(((1, 1), 5))
        self.PAIR = {0: ((0, 0), 0), 2: ((0, 0), 1), 4: ((0, 0), 2), 6: ((0, 0), 3)}
        for n, q in enumerate(across):
            self.PAIR[8 + n] = ((2, 0), q)
        self.out, self.own, self.place, self.device = out, own, place, device
        self.send, self.recv, self.sibling = send, recv, sibling
        self.ids_out, self.ids_own, self.ids_place, self.ids_send, self.ids_recv = ids_out, ids_own, ids_place, ids_send, ids_recv
        self.count, self.here, self.ids_here, self.ids_sent = 0, set(), set(), []
        self.lines = {"up": [], "down": [], "pair": []}

    def tile(self, slab, q):
        return self.out.at[self.place(*slab), pl.ds(*PIECES[q])]

    def start(self, line, slab, q, ring, pair):
        sent = self.lines[line]
        if len(sent) >= self.WINDOW:
            sent[-self.WINDOW].wait_send()
        if slab != (0, 0):
            self.arrived(slab, min(q, 2) if q > 3 else q)
        there = ((slab[0] - ring) % 4, (slab[1] - pair) % 2)
        source = self.own.at[pl.ds(*PIECES[q])] if slab == (0, 0) else self.tile(slab, q)
        copy = pltpu.make_async_remote_copy(
            src_ref=source,
            dst_ref=self.tile(slab, q),
            send_sem=self.send.at[self.count],
            recv_sem=self.recv.at[(there[0] + 4 * there[1]) * len(PIECES) + q],
            device_id=self.device(ring, pair),
            device_id_type=MESH,
        )
        copy.start()
        self.count += 1
        sent.append(copy)

    def start_ids(self, slab, ring, pair):
        there = ((slab[0] - ring) % 4, (slab[1] - pair) % 2)
        if slab != (0, 0):
            self.ids_arrived(slab)
        copy = pltpu.make_async_remote_copy(
            src_ref=self.ids_own if slab == (0, 0) else self.ids_out.at[self.ids_place(*slab)],
            dst_ref=self.ids_out.at[self.ids_place(*slab)],
            send_sem=self.ids_send.at[len(self.ids_sent)],
            recv_sem=self.ids_recv.at[there[0] + 4 * there[1]],
            device_id=self.device(ring, pair),
            device_id_type=MESH,
        )
        copy.start()
        self.ids_sent.append(copy)

    def ids_arrived(self, slab):
        if slab not in self.ids_here:
            self.ids_here.add(slab)
            here = self.ids_out.at[self.ids_place(*slab)]
            pltpu.make_async_copy(here, here, self.ids_recv.at[slab[0] + 4 * slab[1]]).wait()

    def arrived(self, slab, q):
        if (slab, q) in self.here:
            return
        self.here.add((slab, q))
        here = self.tile(slab, q)
        pltpu.make_async_copy(here, here, self.recv.at[(slab[0] + 4 * slab[1]) * len(PIECES) + q]).wait()
        if self.sibling is not None:
            self.sibling(self, slab, q)

    def tick(self, t):
        if t in self.PAIR:
            self.start("pair", *self.PAIR[t], 0, 1)
        if t < len(self.UP):
            self.start("up", *self.UP[t], 1, 0)
            self.start("down", *self.DOWN[t], 3, 0)
        for way in IDS_TICKS.get(t, ()):
            self.start_ids(*way)
        if 2 <= t < len(self.UP) + 2:
            (ring, pair), q = self.UP[t - 2]
            self.arrived(((ring + 3) % 4, pair), q)
            (ring, pair), q = self.DOWN[t - 2]
            self.arrived(((ring + 1) % 4, pair), q)
        if t - 3 in self.PAIR:
            slab, q = self.PAIR[t - 3]
            self.arrived((slab[0], 1), q)

    def finish(self):
        for line in self.lines.values():
            for copy in line[-self.WINDOW:]:
                copy.wait_send()
        for copy in self.ids_sent:
            copy.wait_send()


def gather_kernel(left, right, left_slots, right_slots, left_all, right_all, all_ids, blank,
                  ids, slots, left_send, left_recv, right_send, right_recv, sib_send, sib_recv,
                  idl_send, idl_recv, idr_send, idr_recv, ids_sib, own_sem):
    row, col = lax.axis_index("row"), lax.axis_index("col")
    y_hi, z = row // 4, lax.rem(row, 4)
    core, x, y_lo = lax.rem(col, 2), lax.rem(col // 2, 4), col // 8

    def left_place(ring, pair):
        return (lax.rem(y_lo + pair, 2) * 4 + lax.rem(x + ring, 4)) * 2 + core

    def right_place(ring, pair):
        return lax.rem(y_hi + pair, 2) * 4 + lax.rem(z + ring, 4)

    other = (row, col + 1 - 2 * core)

    fetch = [
        pltpu.make_async_copy(left_slots, slots.at[pl.ds(0, 1)], own_sem.at[4]),
        pltpu.make_async_copy(right_slots, slots.at[pl.ds(1, 1)], own_sem.at[5]),
    ]
    for copy in fetch:
        copy.start()
    barrier = pltpu.get_barrier_semaphore()
    for peer in (
        (row, left_place(1, 0)), (row, left_place(3, 0)), (row, left_place(0, 1)), other,
        (right_place(1, 0), col), (right_place(3, 0), col), (right_place(0, 1), col),
    ):
        pl.semaphore_signal(barrier, inc=1, device_id=peer, device_id_type=MESH)

    pl.semaphore_wait(barrier, 7)

    shared = []

    def to_sibling(factor, slab, q):
        index = (slab[0] + 4 * slab[1]) * 4 + q
        part = factor.tile(slab, q)
        copy = pltpu.make_async_remote_copy(
            src_ref=factor.own.at[pl.ds(q * TILE, TILE)] if slab == (0, 0) else part,
            dst_ref=part,
            send_sem=sib_send.at[index],
            recv_sem=sib_recv.at[index],
            device_id=other,
            device_id_type=MESH,
        )
        copy.start()
        shared.append(copy)

    def left_ids_place(ring, pair):
        return core * N_ROW + left_place(ring, pair) // 2

    lf = Factor(
        left_all, left, left_place, lambda ring, pair: (row, left_place(ring, pair)), left_send, left_recv, to_sibling,
        all_ids, ids, left_ids_place, idl_send, idl_recv, (2, 3),
    )
    rf = Factor(
        right_all, right, right_place, lambda ring, pair: (right_place(ring, pair), col), right_send, right_recv, None,
        all_ids, ids, lambda ring, pair: N_COL + right_place(ring, pair), idr_send, idr_recv, (3,),
    )

    lf.tick(0)
    rf.tick(0)

    lane = lax.broadcasted_iota(jnp.int32, (1, LANES), 1)
    for copy in fetch:
        copy.wait()
    row_ids = jnp.full((1, LANES), -1, jnp.int32)
    for s in range(CAP):
        row_ids = jnp.where(lane == s, slots[0, s], row_ids)
        row_ids = jnp.where(lane == CAP + s, slots[1, s], row_ids)
    ids[...] = row_ids

    lf.tick(1)
    rf.tick(1)

    for q in range(CAP):
        to_sibling(lf, (0, 0), q)
    local = [
        pltpu.make_async_copy(left, left_all.at[col], own_sem.at[0]),
        pltpu.make_async_copy(right, right_all.at[row], own_sem.at[1]),
        pltpu.make_async_copy(ids, all_ids.at[left_ids_place(0, 0)], own_sem.at[2]),
        pltpu.make_async_copy(ids, all_ids.at[N_COL + row], own_sem.at[3]),
    ]
    for copy in local:
        copy.start()

    @pl.loop(0, EXPANDED[0])
    def _(n):
        blank[n] = jnp.zeros(EXPANDED[1:], jnp.float32)

    slabs = [(ring, pair) for pair in range(2) for ring in range(4)][1:]
    for t in range(2, 14):
        lf.tick(t)
        if t == 10:
            for copy in local:
                copy.wait()
            for slab in slabs:
                lf.ids_arrived(slab)
            block = all_ids.at[pl.ds(core * N_ROW, N_ROW)]
            copy = pltpu.make_async_remote_copy(
                src_ref=block, dst_ref=block, send_sem=ids_sib.at[0], recv_sem=ids_sib.at[1], device_id=other, device_id_type=MESH)
            copy.start()
            shared.append(copy)
        rf.tick(t)
    for slab in slabs:
        rf.ids_arrived(slab)

    for index in range(8 * CAP):
        ring, pair, q = index // 4 % 4, index // 16, index % 4
        place = left_place(ring, pair) + 1 - 2 * core
        part = left_all.at[place, pl.ds(q * TILE, TILE)]
        pltpu.make_async_copy(part, part, sib_recv.at[index]).wait()
    theirs = all_ids.at[pl.ds((1 - core) * N_ROW, N_ROW)]
    pltpu.make_async_copy(theirs, theirs, ids_sib.at[1]).wait()
    for copy in shared:
        copy.wait_send()
    lf.finish()
    rf.finish()


def gather(left, right, left_slots, right_slots):
    dma = pltpu.SemaphoreType.DMA
    operands = [pltpu.with_memory_space_constraint(x, pltpu.HBM) for x in (left, right, left_slots, right_slots)]
    return pl.pallas_call(
        gather_kernel,
        out_shape=[
            jax.ShapeDtypeStruct((N_COL, SLAB, TILE), jnp.bfloat16),
            jax.ShapeDtypeStruct((N_ROW, SLAB, TILE), jnp.bfloat16),
            jax.ShapeDtypeStruct((N_COL + N_ROW, 1, LANES), jnp.int32),
            pltpu.VMEM(EXPANDED, jnp.float32),
        ],
        in_specs=[ANY, ANY, ANY, ANY],
        out_specs=[ANY, ANY, ANY, VMEM],
        scratch_shapes=[
            pltpu.VMEM((1, LANES), jnp.int32),
            pltpu.SMEM((2, CAP), jnp.int32),
            dma((28,)), dma((48,)), dma((29,)), dma((48,)), dma((32,)), dma((32,)),
            dma((7,)), dma((8,)), dma((7,)), dma((8,)), dma((2,)), dma((6,)),
        ],
        compiler_params=pltpu.CompilerParams(collective_id=0, has_side_effects=True, vmem_limit_bytes=2**20),
        name="gather_slabs",
    )(*operands)


PER_STEP = 8
HALF = TILE // 2


def product_kernel(all_ids, left_all, right_all, blank, expanded):
    def inner(n, _):
        work = []
        for w in range(PER_STEP):
            q, s = n * (PER_STEP // CAP) + w // CAP, w % CAP
            held = all_ids[N_COL + q, 0, CAP + s]
            kept = held >= 0
            held = jnp.where(kept, held, 0)
            parity = held // CB_DEV
            rows = []
            for u in range(CAP):
                i = all_ids[parity * N_ROW + q, 0, u]
                rows.append(jnp.where(kept & (i >= 0), i, RB_DEV))
            work.append((q, s, 2 * q + parity, lax.rem(held, CB_DEV), rows))
        for q, s, k, j, rows in work:
            weights = right_all[q, s * TILE : (s + 1) * TILE]
            for u, i in enumerate(rows):
                for h in range(TILE // HALF):
                    expanded[i * CB_DEV + j, h * HALF : (h + 1) * HALF] += jnp.dot(
                        left_all[k, u * TILE + h * HALF : u * TILE + (h + 1) * HALF], weights, preferred_element_type=jnp.float32
                    )
        return 0

    lax.fori_loop(0, N_ROW * CAP // PER_STEP, inner, 0)


def product(all_ids, left_all, right_all, blank):
    return pl.pallas_call(
        product_kernel,
        out_shape=pltpu.VMEM(EXPANDED, jnp.float32),
        in_specs=[SMEM, VMEM, VMEM, VMEM],
        out_specs=VMEM,
        input_output_aliases={3: 0},
        compiler_params=pltpu.CompilerParams(vmem_limit_bytes=4 * 2**20),
        name="tile_products",
    )(all_ids, left_all, right_all, blank)


def total_kernel(expanded, total, part, held, send, recv):
    row, col = lax.axis_index("row"), lax.axis_index("col")
    peers = [(lax.rem(row + step, N_ROW), col) for step in range(1, N_ROW)]
    barrier = pltpu.get_barrier_semaphore()
    for peer in peers:
        pl.semaphore_signal(barrier, inc=1, device_id=peer, device_id_type=MESH)

    for j in range(CB_DEV):

        def add(i, sums):
            rows = expanded[i * CB_DEV + j]
            return sums + jnp.sum((rows * rows).reshape(TILE // 16, 16, TILE), axis=0)

        sums = lax.fori_loop(0, RB_DEV, add, jnp.zeros((16, TILE), jnp.float32))
        part[:, j * TILE : (j + 1) * TILE] = jnp.sum(sums, axis=0, keepdims=True)
    pl.semaphore_wait(barrier, N_ROW - 1)
    copies = []
    for n, peer in enumerate(peers):
        copy = pltpu.make_async_remote_copy(
            src_ref=part, dst_ref=held.at[n], send_sem=send.at[n], recv_sem=recv.at[n],
            device_id=peer, device_id_type=MESH)
        copy.start()
        copies.append(copy)
    value = part[...]
    for n, copy in enumerate(copies):
        copy.wait_recv()
        value = value + held[n]
    total[...] = value
    for copy in copies:
        copy.wait_send()


def column_total(expanded):
    dma = pltpu.SemaphoreType.DMA
    shape = (1, CB_DEV * TILE)
    return pl.pallas_call(
        total_kernel,
        out_shape=jax.ShapeDtypeStruct(shape, jnp.float32),
        in_specs=[VMEM],
        out_specs=VMEM,
        scratch_shapes=[
            pltpu.VMEM(shape, jnp.float32), pltpu.VMEM((N_ROW - 1, *shape), jnp.float32), dma((N_ROW - 1,)), dma((N_ROW - 1,)),
        ],
        compiler_params=pltpu.CompilerParams(collective_id=1, has_side_effects=True, vmem_limit_bytes=2**20),
        name="column_total",
    )(expanded)


SCALE_BLOCKS = [TILE] * RB_DEV
SCALE_SLOTS = 8


def scale_kernel(total, expanded, out, scaled, sems):
    factor = 1.0 / (total[...] / (RB_DEV * TILE * N_ROW) + EPSILON)
    copies, done = [], 0
    for n, count in enumerate(SCALE_BLOCKS):
        slot = n % SCALE_SLOTS
        if n >= SCALE_SLOTS:
            copies[n - SCALE_SLOTS].wait()
        i, first = done // TILE, done % TILE
        for j in range(CB_DEV):
            columns = slice(j * TILE, (j + 1) * TILE)
            value = expanded[i * CB_DEV + j, first : first + count]
            scaled[slot, :count, columns] = value * value * factor[:, columns]
        copy = pltpu.make_async_copy(scaled.at[slot, pl.ds(0, count)], out.at[pl.ds(done, count)], sems.at[slot])
        copy.start()
        copies.append(copy)
        done += count
    for copy in copies[-SCALE_SLOTS:]:
        copy.wait()


def scale(total, expanded):
    rows, cols = RB_DEV * TILE, CB_DEV * TILE
    return pl.pallas_call(
        scale_kernel,
        out_shape=jax.ShapeDtypeStruct((rows, cols), jnp.float32),
        in_specs=[VMEM, VMEM],
        out_specs=ANY,
        scratch_shapes=[pltpu.VMEM((SCALE_SLOTS, TILE, cols), jnp.float32), pltpu.SemaphoreType.DMA((SCALE_SLOTS,))],
        compiler_params=pltpu.CompilerParams(vmem_limit_bytes=10 * 2**20),
        name="scale_columns",
    )(total, expanded)


def body(left_tiles, left_slots, right_tiles, right_slots):
    left = left_tiles.reshape(SLAB, TILE)
    right = right_tiles.reshape(SLAB, TILE)
    left_all, right_all, all_ids, blank = gather(
        left, right, left_slots.reshape(1, CAP), right_slots.reshape(1, CAP)
    )
    expanded = product(all_ids, left_all, right_all, blank)
    return scale(column_total(expanded), expanded)


def solution(mesh):
    placed = (P("row", "col", None), P("row", "col"), P("row", "col", None), P("row", "col"))
    return jax.shard_map(
        body, mesh=mesh, in_specs=placed, out_specs=P("row", "col"), check_vma=False
    )
```
